256 devices in a mesh: row: 32 (over x, z), col: 8 (over y, core).
Axes of the slice: x: 4, y: 4, z: 8, core: 2. Of those that a mesh axis runs over, the one named last changes fastest.
Arguments:
- trailing: float32 [2, 12288, 12288], P(None, 'row', 'col'), may hold values from -6 to 6
- panel: bfloat16 [2, 12288, 512], P(None, ('row', 'col')), may hold values from -1.296875 to 1.296875
- diagonal: float32 [2, 512, 512], replicated, as said below
- pattern: int32 [96], replicated, may hold values 0 or 1
Outputs:
- updated: float32 [2, 12288, 12288], P(None, 'row', 'col')
- solved: float32 [2, 12288, 512], P(None, ('row', 'col'))
The draws below stay inside these ranges and needn't reach their ends.
Inputs may be any that keep to these rules, and one draw needn't show every extreme that they name: symmetric; each diagonal entry exceeds the sum of magnitudes of the other entries of its row by 0.2 or more.
All inputs are finite; a program needn't handle non-finite values.
Results may differ from the reference program's by a relative error of at most 0.0003.
Values may be sent and summed in bfloat16 or wider, within the bound.
A program may use at most 128 MiB of HBM per device.

```python
import jax
import jax.numpy as jnp
from jax import lax

BLK = 128
SUPER = 512
N = 12288
NB = 96


def draw_diagonal(key, part):
    key = jax.random.fold_in(key, 5)
    first, second = jax.random.split(key)
    unit = jnp.eye(SUPER, dtype=jnp.float32)
    others = 1.0 - unit
    strength = jax.random.uniform(first, (2, SUPER, SUPER), jnp.float32, -0.4, 1.0) * (2.3 / (SUPER - 1))
    center = jax.random.uniform(second, (2, SUPER), jnp.float32, 2.5, 4.0)
    mirror = 0.5 * (strength + jnp.swapaxes(strength, 1, 2))
    return center[:, :, None] * unit - mirror * others


def touch_ends(array, stream_key, smallest, top_value):
    index_at = [jax.random.randint(jax.random.fold_in(stream_key, axis), (), 0, length) for axis, length in enumerate(array.shape)]
    longest = array.shape.index(max(array.shape))
    beside = index_at[:longest] + [(index_at[longest] + 1) % array.shape[longest]] + index_at[longest + 1:]
    return array.at[tuple(index_at)].set(smallest).at[tuple(beside)].set(top_value)


def level_of(stream_key, extent, pieces, low, largest):
    loudness, own = 1.0, jax.random.fold_in(stream_key, 6)
    for axis_at, blocks in pieces:
        steps = jnp.exp(jax.random.uniform(jax.random.fold_in(own, axis_at), (blocks,), jnp.float32, low / len(pieces), largest / len(pieces)))
        loudness = loudness * jnp.repeat(steps, extent[axis_at] // blocks).reshape([-1 if axis == axis_at else 1 for axis in range(len(extent))])
    return loudness


def noise(rng, shape, deviation, limit, pieces=(), held_as=jnp.bfloat16):
    array = deviation * jax.random.normal(rng, shape, jnp.float32)
    if pieces:
        array = array * level_of(rng, shape, pieces, -0.22, 0.18)
    return jnp.clip(array, -limit, limit).astype(held_as)


def setup_inputs(seed: int = 0) -> dict:
    arg_keys = jax.random.split(jax.random.key(seed), 5)
    trailing = noise(arg_keys[0], (2, N, N), 1.0, 6.0, ((1, 32), (2, 8)), jnp.float32)
    panel = noise(arg_keys[1], (2, N, SUPER), 0.21, 1.296875, ((1, 256),))
    diagonal = draw_diagonal(jax.random.fold_in(arg_keys[4], 71), 0)
    pattern = touch_ends((jax.random.randint(arg_keys[3], (NB,), 0, 4) < 3).astype(jnp.int32), jax.random.fold_in(arg_keys[3], 1), 0, 1)
    return dict(trailing=trailing, panel=panel, diagonal=diagonal, pattern=pattern)


def reference(trailing, panel, diagonal, pattern):
    keep = jnp.repeat(pattern, BLK).astype(jnp.float32)
    updated_list = []
    solved_list = []
    for band in range(2):
        factor = jnp.linalg.cholesky(diagonal[band])
        inverse = jax.scipy.linalg.solve_triangular(factor, jnp.eye(SUPER, dtype=diagonal.dtype), lower=True)
        solved = jnp.dot(panel[band].astype(jnp.float32), inverse.T, precision=lax.Precision.HIGHEST) * keep[:, None]
        rounded = solved.astype(jnp.bfloat16)
        update = jnp.dot(rounded.astype(jnp.float32), rounded.T.astype(jnp.float32), preferred_element_type=jnp.float32)
        updated_list.append(trailing[band] - update)
        solved_list.append(solved)
    return (jnp.stack(updated_list), jnp.stack(solved_list))
```

```python
import jax, jax.numpy as jnp
from jax import lax
from jax.experimental import pallas as pl
from jax.experimental.pallas import tpu as pltpu
from jax.sharding import PartitionSpec as P

BLK = 128
F32=jnp.float32
HI=lax.Precision.HIGHEST

def dot(a,b,ca,cb):
    return lax.dot_general(a,b,(((ca,),(cb,)),((),())),precision=HI,preferred_element_type=F32)

def bc(x,k):
    return jnp.broadcast_to(x[k:k+1,:],(8,128))

def base(X):
    lane = lax.broadcasted_iota(jnp.int32,(8,128),1)
    sub = lax.broadcasted_iota(jnp.int32,(8,128),0)
    half = jnp.where(lane<64,0,64)
    l64 = lane-half
    E=[jnp.where(l64==sub+8*g,1.0,0.0).astype(F32) for g in range(8)]
    X=list(X)
    out=[]
    for p in range(8):
        T={}
        for g in range(p,8):
            T[g]=[jnp.take_along_axis(X[g],half+(8*p+c),axis=1,mode="promise_in_bounds") for c in range(8)]
        dv=T[p][0]
        for k in range(8):
            d=bc(T[p][k],k)
            dv=jnp.where(sub==k,d,dv)
            r=1.0/d
            pe=bc(E[p],k)
            px=bc(X[p],k)
            tr={c:bc(T[p][c],k) for c in range(k+1,8)}
            for g in range(p,8):
                m=T[g][k]*r
                if g==p:
                    if k==7: continue
                    m=jnp.where(sub>k,m,0.0)
                for c in range(k+1,8):
                    T[g][c]=T[g][c]-m*tr[c]
                if p<7: X[g]=X[g]-m*px
                E[g]=E[g]-m*pe
        out.append(E[p]*lax.rsqrt(dv))
    return out

def chol_kernel(d_ref, hi_ref, mid_ref, lo_ref, W):
    for b in range(2):
        W[b]=d_ref[b]
    lane=lax.broadcasted_iota(jnp.int32,(8,128),1)
    lane512=lax.broadcasted_iota(jnp.int32,(64,512),1)
    def step(t, carry):
        o=pl.multiple_of(t*128,128)
        for s in range(2):
            os=pl.multiple_of(o+64*s,64)
            X=[]
            for g in range(8):
                a0=W[0,pl.ds(pl.multiple_of(os+8*g,8),8),pl.ds(o,128)]
                a1=W[1,pl.ds(pl.multiple_of(os+8*g,8),8),pl.ds(o,128)]
                if s==0: X.append(jnp.where(lane<64,a0,pltpu.roll(a1,64,1)))
                else: X.append(jnp.where(lane<64,pltpu.roll(a0,64,1),a1))
            Y=jnp.concatenate(base(X),axis=0)
            for b in range(2):
                Yb=Y[:,64*b:64*b+64]
                V=W[b,pl.ds(os,64),:]
                Vn=dot(Yb,V,1,0)
                Yt=jnp.concatenate([Yb,Yb]*4,axis=1)
                injj=(lane512>=os)&(lane512<os+64)
                Vn=jnp.where(injj,Yt,Vn)
                W[b,pl.ds(os,64),:]=Vn
                def chunk(i,c):
                    ro=pl.multiple_of(i*128,128)
                    L=W[b,pl.ds(ro,128),pl.ds(o,128)][:,64*s:64*s+64]
                    Ln=dot(L,Yb,1,1)
                    row=lax.broadcasted_iota(jnp.int32,(128,64),0)+ro
                    Ln=jnp.where(row>=os+64,Ln,0.0)
                    rr=lax.broadcasted_iota(jnp.int32,(128,512),0)+ro
                    ll=lax.broadcasted_iota(jnp.int32,(128,512),1)
                    old=W[b,pl.ds(ro,128),:]
                    old=jnp.where((rr>=os+64)&(ll>=os)&(ll<os+64),0.0,old)
                    W[b,pl.ds(ro,128),:]=old-dot(Ln,Vn,1,0)
                    return c
                lax.fori_loop(t if s==0 else t+1,4,chunk,0)
        return carry
    lax.fori_loop(0,4,step,0)
    for b in range(2):
        r=lax.broadcasted_iota(jnp.int32,(512,512),0)
        l=lax.broadcasted_iota(jnp.int32,(512,512),1)
        y=jnp.where(r>=l,W[b],0.0)
        hi=y.astype(jnp.bfloat16)
        y=y-hi.astype(F32)
        mid=y.astype(jnp.bfloat16)
        lo=(y-mid.astype(F32)).astype(jnp.bfloat16)
        hi_ref[b]=hi
        mid_ref[b]=mid
        lo_ref[b]=lo

def cholinv(d):
    return pl.pallas_call(chol_kernel,out_shape=[jax.ShapeDtypeStruct(d.shape,jnp.bfloat16)]*3,name="cholinv",
      scratch_shapes=[pltpu.VMEM(d.shape,F32)],
      cost_estimate=pl.CostEstimate(flops=20*10**9,bytes_accessed=5*10**6,transcendentals=0),
      compiler_params=pltpu.CompilerParams(vmem_limit_bytes=48<<20))(d)


def solve_rows(p, y_refs, b):
    half = p.shape[1] // 2
    parts = []
    for lo, depth in ((0, half), (half, 2 * half)):
        acc = None
        for y in y_refs:
            term = lax.dot_general(
                p[:, :depth],
                y[b, lo : lo + half, :depth],
                (((1,), (1,)), ((), ())),
                preferred_element_type=F32,
            )
            acc = term if acc is None else acc + term
        parts.append(acc)
    return jnp.concatenate(parts, axis=1)


def keep_rows(x, pat_ref, first_block):
    blocks = [
        x[i * BLK : (i + 1) * BLK] * pat_ref[first_block + i].astype(F32)
        for i in range(x.shape[0] // BLK)
    ]
    return jnp.concatenate(blocks, axis=0)


def update_kernel(pat_ref, own_ref, row_ref, col_ref, hi_ref, mid_ref, lo_ref, trail_ref, out_ref, solved_ref, rows):
    b = pl.program_id(0)
    tile = pl.program_id(1)
    row, col = lax.axis_index("row"), lax.axis_index("col")
    ys = (hi_ref, mid_ref, lo_ref)

    @pl.when(tile == 0)
    def _():
        r = solve_rows(row_ref[0], ys, b)
        rows[...] = keep_rows(r, pat_ref, row * 3).astype(jnp.bfloat16)
        own = solve_rows(own_ref[0], ys, b)
        first = (row * 8 + col) * 48
        low = first // BLK
        high = (first + 47) // BLK
        at = first + lax.broadcasted_iota(jnp.int32, own.shape, 0)
        keep = jnp.where(at < high * BLK, pat_ref[low], pat_ref[high]).astype(F32)
        solved_ref[0] = own * keep

    c = solve_rows(col_ref[0], ys, b)
    per = col_ref.shape[1] // BLK
    c = keep_rows(c, pat_ref, col * 12 + tile * per).astype(jnp.bfloat16)
    out_ref[0] = trail_ref[0] - lax.dot_general(
        rows[...], c, (((1,), (1,)), ((), ())), preferred_element_type=F32
    )


def update(pattern, own, rowp, colp, ys, trailing):
    nb, m, n = trailing.shape
    width = 512
    k = own.shape[2]
    whole = pl.BlockSpec((nb, k, k), lambda b, t: (0, 0, 0))
    return pl.pallas_call(
        update_kernel,
        grid=(nb, n // width),
        in_specs=[
            pl.BlockSpec(memory_space=pltpu.SMEM),
            pl.BlockSpec((1, own.shape[1], k), lambda b, t: (b, 0, 0)),
            pl.BlockSpec((1, m, k), lambda b, t: (b, 0, 0)),
            pl.BlockSpec((1, width, k), lambda b, t: (b, t, 0)),
            whole,
            whole,
            whole,
            pl.BlockSpec((1, m, width), lambda b, t: (b, 0, t)),
        ],
        out_specs=[
            pl.BlockSpec((1, m, width), lambda b, t: (b, 0, t)),
            pl.BlockSpec((1, own.shape[1], k), lambda b, t: (b, 0, 0)),
        ],
        out_shape=[
            jax.ShapeDtypeStruct(trailing.shape, F32),
            jax.ShapeDtypeStruct(own.shape, F32),
        ],
        scratch_shapes=[pltpu.VMEM((m, k), jnp.bfloat16)],
        compiler_params=pltpu.CompilerParams(vmem_limit_bytes=48 << 20),
        cost_estimate=pl.CostEstimate(flops=6 * 10**9, bytes_accessed=16 * 10**6, transcendentals=0),
        name="solve_update",
    )(pattern, own, rowp, colp, *ys, trailing)


def per_device(trailing, panel, diagonal, pattern):
    n_row = lax.axis_size("row")
    n_col = lax.axis_size("col")
    ratio = n_row // n_col
    perm = [
        (r * n_col + c, ((r % ratio) * n_col + c) * n_col + r // ratio)
        for r in range(n_row)
        for c in range(n_col)
    ]
    moved = lax.ppermute(panel, ("row", "col"), perm)
    rowp = lax.all_gather(panel, "col", axis=1, tiled=True)
    colp = lax.all_gather(moved, "row", axis=1, tiled=True)
    ys = cholinv(diagonal)
    return tuple(update(pattern, panel, rowp, colp, ys, trailing))


def solution(mesh):
    return jax.shard_map(
        per_device,
        mesh=mesh,
        in_specs=(P(None, "row", "col"), P(None, ("row", "col"), None), P(), P()),
        out_specs=(P(None, "row", "col"), P(None, ("row", "col"), None)),
        check_vma=False,
    )
```

```python
import functools

import jax
import jax.numpy as jnp
from jax import lax
from jax.experimental import pallas as pl
from jax.experimental.pallas import tpu as pltpu
from jax.sharding import PartitionSpec as P

BLK = 128
F32 = jnp.float32
BF = jnp.bfloat16
HIGHEST = lax.Precision.HIGHEST
MESH = pl.DeviceIdType.MESH
NX, NZ, NC = 4, 8, 8

PLAN = {
    11: [('A', 0, 0), ('B', 0, 0)],
    19: [('A', 1, 0), ('A', -1, 0), ('A', 0, 1), ('A', 0, -1)],
    21: [('B', 1, 0), ('B', -1, 0), ('B', 0, 1), ('B', 0, -1)],
    25: [('A', 2, 0)],
    30: [('A', 1, 1), ('A', -1, 1), ('A', 0, 2), ('A', 1, -1), ('A', -1, -1), ('A', 0, -2)],
    33: [('B', -1, 1), ('B', -1, -1), ('A', 2, 1), ('A', 2, -1)],
    34: [('B', 0, 2), ('B', 0, -2)],
    36: [('B', 2, 0), ('B', 1, 1), ('B', 1, -1)],
    41: [('A', 1, 2), ('A', -1, 2), ('A', 0, 3), ('A', 1, -2), ('A', -1, -2), ('A', 0, -3)],
    43: [('A', 2, 2), ('A', 2, -2)],
    45: [('B', 0, 3), ('B', 0, -3)],
    46: [('B', 1, 2), ('B', 1, -2)],
    50: [('A', 1, -3), ('A', -1, -3)],
    51: [('A', 2, -3), ('B', 2, 1), ('B', 2, -1)],
    53: [('A', 1, 3), ('A', -1, 3), ('A', 0, 4), ('B', -1, 2), ('B', -1, -2)],
    54: [('A', 2, 3)],
    56: [('B', 0, 4)],
    57: [('A', -1, 4)],
    58: [('A', 2, 4)],
    59: [('B', -1, 3), ('B', -1, -3), ('A', 1, 4)],
    63: [('B', 1, 3), ('B', 1, -3)],
    64: [('B', 2, 2), ('B', 2, -2), ('B', -1, 4), ('B', 1, 4), ('B', 2, 3), ('B', 2, -3), ('B', 2, 4)],
}
PART = {"A": (0, 16), "B": (16, 32)}


def onward(part, dx, dz):
    out = []
    along_x = part == "B" or dz == 0
    along_z = part == "A" or dx == 0
    if along_x:
        if dx == 0:
            out += [("x", 1, 1, dz), ("x", -1, -1, dz)]
        elif dx == 1 and (part == "A" or dz % 2 == 0):
            out += [("x", 1, 2, dz)]
        elif dx == -1 and part == "B" and dz % 2 == 1:
            out += [("x", -1, 2, dz)]
    if along_z:
        if dz == 0:
            out += [("z", 1, dx, 1), ("z", -1, dx, -1)]
        elif 0 < dz < 3 or (dz == 3 and (part == "B" or dx in (0, 1))):
            out += [("z", 1, dx, dz + 1)]
        elif -3 < dz < 0 or (dz == -3 and part == "A" and dx in (2, -1)):
            out += [("z", -1, dx, dz - 1 if dz > -3 else 4)]
    return out


def rel(dx, dz):
    return (dx % NX) * NZ + dz % NZ


class Gather:
    def __init__(self, panel, cols, rows, first_sem, arrive_sem, send_sem, recv_sem, row_send, row_recv, own_sem):
        self.panel, self.cols, self.rows = panel, cols, rows
        self.first_sem, self.arrive_sem = first_sem, arrive_sem
        self.send_sem, self.recv_sem = send_sem, recv_sem
        self.row_send, self.row_recv, self.own_sem = row_send, row_recv, own_sem
        self.row, self.col = lax.axis_index("row"), lax.axis_index("col")
        self.x, self.z = self.row // NZ, self.row % NZ
        self.y, self.k = self.col // 2, self.col % 2
        x, y, z, k = self.x, self.y, self.z, self.k
        self.to_row = ((x + y) % NX) * NZ + (2 * (z % 4) + k + 6 + 4 * (z // 4)) % NZ
        self.to_col = 2 * x + z // 4
        self.to_slot = (z % 4) * NC + self.col
        u = (z + 10 - 4 * k) % NZ
        self.from_row = y * NZ + 4 * k + u // 2
        self.from_col = ((x + NX - y) % NX) * 2 + u % 2
        self.stays = (self.to_row == self.row) & (self.to_col == self.col)
        self.moves = jnp.logical_not(self.stays)
        self.home = self.slot(0, 0)
        self.sent = []

    def slot(self, dx, dz):
        xh = (self.x - dx + 2 * NX) % NX
        u = (self.z - dz + 2 * NZ + 10 - 4 * self.k) % NZ
        return (u // 2) * NC + ((xh + NX - self.y) % NX) * 2 + u % 2

    def neighbour(self, axis, step):
        if axis == "x":
            return (((self.x + step + NX) % NX) * NZ + self.z, self.col)
        return (self.x * NZ + (self.z + step + NZ) % NZ, self.col)

    def peer(self, i):
        return (self.row, (self.col + i) % NC)

    def barrier(self):
        sem = pltpu.get_barrier_semaphore()
        near = [self.neighbour(a, s) for a in "xz" for s in (1, -1)]
        near += [self.peer(i) for i in range(1, NC)]
        for d in near:
            pl.semaphore_signal(sem, inc=1, device_id=d, device_id_type=MESH)

        @pl.when(self.moves)
        def _():
            for d in ((self.to_row, self.to_col), (self.from_row, self.from_col)):
                pl.semaphore_signal(sem, inc=1, device_id=d, device_id_type=MESH)
            pl.semaphore_wait(sem, len(near) + 2)

        pl.when(self.stays)(lambda: pl.semaphore_wait(sem, len(near)))

    def first(self, slot):
        return pltpu.make_async_remote_copy(
            self.panel, self.cols.at[:, slot], self.first_sem, self.arrive_sem,
            device_id=(self.to_row, self.to_col), device_id_type=MESH,
        )

    def first_stays(self):
        return pltpu.make_async_copy(self.panel, self.cols.at[:, self.home], self.first_sem)

    def row_copy(self, i, col):
        return pltpu.make_async_remote_copy(
            self.panel, self.rows.at[:, col], self.row_send.at[i], self.row_recv.at[i],
            device_id=self.peer(i + 1), device_id_type=MESH,
        )

    def row_own(self):
        return pltpu.make_async_copy(self.panel, self.rows.at[:, self.col], self.own_sem)

    def start(self):
        pl.when(self.moves)(lambda: self.first(self.to_slot).start())
        pl.when(self.stays)(lambda: self.first_stays().start())
        for i in range(NC - 1):
            self.row_copy(i, self.col).start()
        self.row_own().start()

    def piece(self, part, slot):
        return self.cols.at[:, slot, pl.ds(*PART[part])]

    def move(self, part, slot, i, dx, dz, to):
        ref = self.piece(part, slot)
        return pltpu.make_async_remote_copy(
            ref, ref, self.send_sem.at[i], self.recv_sem.at[0 if part == "A" else 1, rel(dx, dz)],
            device_id=to, device_id_type=MESH,
        )

    def arrival(self, part, dx, dz):
        slot = self.slot(dx, dz)
        if (dx, dz) != (0, 0):
            self.move(part, slot, 0, dx, dz, self.neighbour("x", 1)).wait_recv()
        elif part == "A":
            pl.when(self.moves)(lambda: self.first(self.home).wait_recv())
            pl.when(self.stays)(lambda: self.first_stays().wait())
        for axis, step, ndx, ndz in onward(part, dx, dz):
            self.move(part, slot, len(self.sent), ndx, ndz, self.neighbour(axis, step)).start()
            self.sent.append(part)

    def point(self, h):
        for part, dx, dz in PLAN.get(h, ()):
            self.arrival(part, dx, dz)

    def wait_rows(self):
        for i in range(NC - 1):
            self.row_copy(i, (self.col + NC - 1 - i) % NC).wait_recv()
        self.row_own().wait()

    def drain(self):
        for i, part in enumerate(self.sent):
            self.move(part, self.home, i, 0, 0, self.neighbour("x", 1)).wait_send()
        pl.when(self.moves)(lambda: self.first(self.to_slot).wait_send())
        for i in range(NC - 1):
            self.row_copy(i, self.col).wait_send()


DMA = pltpu.SemaphoreType.DMA
GATHER_SEMS = [DMA, DMA, DMA((62,)), DMA((2, NX * NZ)), DMA((NC - 1,)), DMA((NC - 1,)), DMA]


def dot(a, b, ca, cb, precision=None):
    return lax.dot_general(
        a, b, (((ca,), (cb,)), ((), ())), precision=precision, preferred_element_type=F32
    )


def split3(x):
    hi = x.astype(BF)
    rest = x - hi.astype(F32)
    mid = rest.astype(BF)
    return hi, mid, (rest - mid.astype(F32)).astype(BF)


def stack6(x, axis, left):
    h, m, l = split3(x)
    return jnp.concatenate([h, h, m, h, l, m] if left else [h, m, h, l, h, m], axis=axis)


def spread(x, k):
    return jnp.broadcast_to(x[k : k + 1, :], (8, 128))


def base(x, point):
    lane = lax.broadcasted_iota(jnp.int32, (8, 128), 1)
    sub = lax.broadcasted_iota(jnp.int32, (8, 128), 0)
    half = jnp.where(lane < 64, 0, 64)
    x = list(x)
    e = [jnp.where(lane - half == sub + 8 * g, 1.0, 0.0).astype(F32) for g in range(8)]
    out = []
    for p in range(8):
        point(p)
        t = {
            g: [
                jnp.take_along_axis(x[g], half + (8 * p + c), axis=1, mode="promise_in_bounds")
                for c in range(8)
            ]
            for g in range(p, 8)
        }
        pivots = t[p][0]
        for k in range(8):
            d = spread(t[p][k], k)
            pivots = jnp.where(sub == k, d, pivots)
            r = 1.0 / d
            pe, px = spread(e[p], k), spread(x[p], k)
            top = {c: spread(t[p][c], k) for c in range(k + 1, 8)}
            for g in range(p, 8):
                if g == p and k == 7:
                    continue
                m = t[g][k] * r
                if g == p:
                    m = jnp.where(sub > k, m, 0.0)
                for c in range(k + 1, 8):
                    t[g][c] = t[g][c] - m * top[c]
                if p < 7:
                    x[g] = x[g] - m * px
                e[g] = e[g] - m * pe
        out.append(e[p] * lax.rsqrt(pivots))
    return jnp.concatenate(out, axis=0)


def factor(diag_ref, w, v, s6, point):
    for b in range(2):
        w[b] = diag_ref[b]
    lane = lax.broadcasted_iota(jnp.int32, (8, 128), 1)
    wide = lax.broadcasted_iota(jnp.int32, (64, 512), 1)
    wide2 = lax.broadcasted_iota(jnp.int32, (128, 512), 1)

    def step(t, carry):
        o = pl.multiple_of(t * 128, 128)
        for s in range(2):
            at = pl.multiple_of(o + 64 * s, 64)
            x = []
            for g in range(8):
                rows = pl.ds(pl.multiple_of(at + 8 * g, 8), 8)
                a, b = w[0, rows, pl.ds(o, 128)], w[1, rows, pl.ds(o, 128)]
                if s == 0:
                    x.append(jnp.where(lane < 64, a, pltpu.roll(b, 64, 1)))
                else:
                    x.append(jnp.where(lane < 64, pltpu.roll(a, 64, 1), b))
            y = base(x, functools.partial(point, t, s))
            here = (wide >= at) & (wide < at + 64)
            for b in range(2):
                yb = y[:, 64 * b : 64 * b + 64]
                new = dot(yb, w[b, pl.ds(at, 64), :], 1, 0, HIGHEST)
                new = jnp.where(here, jnp.concatenate([yb] * 8, axis=1), new)
                w[b, pl.ds(at, 64), :] = jnp.where(wide < at + 64, new, 0.0)
                if s == 0:
                    v[b, 0:64, :] = jnp.where((wide >= at + 64) & (wide < at + 128), 0.0, new)
                    below = w[b, pl.ds(at + 64, 64), pl.ds(o, 128)][:, 0:64]
                    lower = dot(below, yb, 1, 1, HIGHEST)
                    rest = jnp.where(here, 0.0, w[b, pl.ds(at + 64, 64), :])
                    w[b, pl.ds(at + 64, 64), :] = rest - dot(lower, new, 1, 0, HIGHEST)
                else:
                    v[b, 64:128, :] = new
        here = (wide2 >= o) & (wide2 < o + 128)

        @pl.when(t < 3)
        def _():
            for b in range(2):
                s6[b] = stack6(v[b], 0, False)

        def chunk(i, c):
            rows = pl.ds(pl.multiple_of(i * 128, 128), 128)
            for b in range(2):
                lower = v[b, :, rows].T
                rest = jnp.where(here, 0.0, w[b, rows, :])
                w[b, rows, :] = rest - dot(stack6(lower, 1, True), s6[b], 1, 0)
            return c

        lax.fori_loop(t + 1, 4, chunk, 0)
        return carry

    lax.fori_loop(0, 4, step, 0)


def gather_factor_kernel(panel, diag, hi, mid, lo, cols, rows, w, v, s6, *sems):
    gather = Gather(panel, cols, rows, *sems)
    gather.barrier()
    gather.start()

    def point(t, s, p):
        for i in range(4):
            h = (2 * i + s) * 8 + p
            if h in PLAN:
                pl.when(t == i)(functools.partial(gather.point, h))

    factor(diag, w, v, s6, point)
    for b in range(2):
        hi[b], mid[b], lo[b] = split3(w[b])
    gather.point(64)
    gather.wait_rows()
    gather.drain()


def gather_factor(panel, diagonal):
    nb, count, k = panel.shape
    vmem = pl.BlockSpec(memory_space=pltpu.VMEM)
    y = jax.ShapeDtypeStruct(diagonal.shape, BF)
    return pl.pallas_call(
        gather_factor_kernel,
        in_specs=[vmem] * 2,
        out_specs=[vmem] * 5,
        out_shape=[
            y, y, y,
            jax.ShapeDtypeStruct((nb, NX * NZ, count, k), BF),
            jax.ShapeDtypeStruct((nb, NC, count, k), BF),
        ],
        scratch_shapes=[
            pltpu.VMEM(diagonal.shape, F32),
            pltpu.VMEM((2, 128, 512), F32),
            pltpu.VMEM((2, 768, 512), BF),
        ] + GATHER_SEMS,
        compiler_params=pltpu.CompilerParams(
            collective_id=0, has_side_effects=True, vmem_limit_bytes=40 << 20
        ),
        cost_estimate=pl.CostEstimate(flops=10**10, bytes_accessed=10**7, transcendentals=0),
        name="gather_factor",
    )(panel, diagonal)


def solve_rows(p, y_refs, b):
    half = p.shape[1] // 2
    parts = []
    for lo, depth in ((0, half), (half, 2 * half)):
        acc = None
        for y in y_refs:
            term = lax.dot_general(
                p[:, :depth],
                y[b, lo : lo + half, :depth],
                (((1,), (1,)), ((), ())),
                preferred_element_type=F32,
            )
            acc = term if acc is None else acc + term
        parts.append(acc)
    return jnp.concatenate(parts, axis=1)


def keep_rows(x, pat_ref, first_block):
    blocks = [
        x[i * BLK : (i + 1) * BLK] * pat_ref[first_block + i].astype(F32)
        for i in range(x.shape[0] // BLK)
    ]
    return jnp.concatenate(blocks, axis=0)


def update_kernel(pat_ref, own_ref, row_ref, col_ref, hi_ref, mid_ref, lo_ref, trail_ref, out_ref, solved_ref, rows):
    b = pl.program_id(0)
    tile = pl.program_id(1)
    row, col = lax.axis_index("row"), lax.axis_index("col")
    ys = (hi_ref, mid_ref, lo_ref)

    @pl.when(tile == 0)
    def _():
        r = solve_rows(row_ref[0], ys, b)
        rows[...] = keep_rows(r, pat_ref, row * 3).astype(jnp.bfloat16)
        own = solve_rows(own_ref[0], ys, b)
        first = (row * 8 + col) * 48
        low = first // BLK
        high = (first + 47) // BLK
        at = first + lax.broadcasted_iota(jnp.int32, own.shape, 0)
        keep = jnp.where(at < high * BLK, pat_ref[low], pat_ref[high]).astype(F32)
        solved_ref[0] = own * keep

    c = solve_rows(col_ref[0], ys, b)
    per = col_ref.shape[1] // BLK
    c = keep_rows(c, pat_ref, col * 12 + tile * per).astype(jnp.bfloat16)
    out_ref[0] = trail_ref[0] - lax.dot_general(
        rows[...], c, (((1,), (1,)), ((), ())), preferred_element_type=F32
    )


def update(pattern, own, rowp, colp, ys, trailing):
    nb, m, n = trailing.shape
    width = 512
    k = own.shape[2]
    whole = pl.BlockSpec((nb, k, k), lambda b, t: (0, 0, 0))
    return pl.pallas_call(
        update_kernel,
        grid=(nb, n // width),
        in_specs=[
            pl.BlockSpec(memory_space=pltpu.SMEM),
            pl.BlockSpec((1, own.shape[1], k), lambda b, t: (b, 0, 0)),
            pl.BlockSpec((1, m, k), lambda b, t: (b, 0, 0)),
            pl.BlockSpec((1, width, k), lambda b, t: (b, t, 0)),
            whole,
            whole,
            whole,
            pl.BlockSpec((1, m, width), lambda b, t: (b, 0, t)),
        ],
        out_specs=[
            pl.BlockSpec((1, m, width), lambda b, t: (b, 0, t)),
            pl.BlockSpec((1, own.shape[1], k), lambda b, t: (b, 0, 0)),
        ],
        out_shape=[
            jax.ShapeDtypeStruct(trailing.shape, F32),
            jax.ShapeDtypeStruct(own.shape, F32),
        ],
        scratch_shapes=[pltpu.VMEM((m, k), jnp.bfloat16)],
        compiler_params=pltpu.CompilerParams(vmem_limit_bytes=48 << 20),
        cost_estimate=pl.CostEstimate(flops=6 * 10**9, bytes_accessed=16 * 10**6, transcendentals=0),
        name="solve_update",
    )(pattern, own, rowp, colp, *ys, trailing)


def per_device(trailing, panel, diagonal, pattern):
    hi, mid, lo, cols, rows = gather_factor(panel, diagonal)
    nb, _, _, k = cols.shape
    return tuple(update(pattern, panel, rows.reshape(nb, -1, k), cols.reshape(nb, -1, k), (hi, mid, lo), trailing))


def solution(mesh):
    return jax.shard_map(
        per_device,
        mesh=mesh,
        in_specs=(P(None, "row", "col"), P(None, ("row", "col"), None), P(), P()),
        out_specs=(P(None, "row", "col"), P(None, ("row", "col"), None)),
        check_vma=False,
    )
```

```python
import functools

import jax
import jax.numpy as jnp
from jax import lax
from jax.experimental import pallas as pl
from jax.experimental.pallas import tpu as pltpu
from jax.sharding import PartitionSpec as P

BLK = 128
F32 = jnp.float32
BF = jnp.bfloat16
HIGHEST = lax.Precision.HIGHEST
MESH = pl.DeviceIdType.MESH
NX, NZ, NC = 4, 8, 8

PLAN = {
    11: [('A', 0, 0), ('B', 0, 0)],
    19: [('A', 1, 0), ('A', -1, 0), ('A', 0, 1), ('A', 0, -1)],
    21: [('B', 1, 0), ('B', -1, 0), ('B', 0, 1), ('B', 0, -1)],
    25: [('A', 2, 0)],
    30: [('A', 1, 1), ('A', -1, 1), ('A', 0, 2), ('A', 1, -1), ('A', -1, -1), ('A', 0, -2)],
    33: [('B', -1, 1), ('B', -1, -1), ('A', 2, 1), ('A', 2, -1)],
    34: [('B', 0, 2), ('B', 0, -2)],
    36: [('B', 2, 0), ('B', 1, 1), ('B', 1, -1)],
    41: [('A', 1, 2), ('A', -1, 2), ('A', 0, 3), ('A', 1, -2), ('A', -1, -2), ('A', 0, -3)],
    43: [('A', 2, 2), ('A', 2, -2)],
    45: [('B', 0, 3), ('B', 0, -3)],
    46: [('B', 1, 2), ('B', 1, -2)],
    50: [('A', 1, -3), ('A', -1, -3)],
    51: [('A', 2, -3), ('B', 2, 1), ('B', 2, -1)],
    53: [('A', 1, 3), ('A', -1, 3), ('A', 0, 4), ('B', -1, 2), ('B', -1, -2)],
    54: [('A', 2, 3)],
    56: [('B', 0, 4)],
    57: [('A', -1, 4)],
    58: [('A', 2, 4)],
    59: [('B', -1, 3), ('B', -1, -3), ('A', 1, 4)],
    63: [('B', 1, 3), ('B', 1, -3)],
    64: [('B', 2, 2), ('B', 2, -2), ('B', -1, 4), ('B', 1, 4), ('B', 2, 3), ('B', 2, -3), ('B', 2, 4)],
}
LAST = 64
PART = {"A": (0, 16), "B": (16, 32)}


def onward(part, dx, dz):
    out = []
    along_x = part == "B" or dz == 0
    along_z = part == "A" or dx == 0
    if along_x:
        if dx == 0:
            out += [("x", 1, 1, dz), ("x", -1, -1, dz)]
        elif dx == 1 and (part == "A" or dz % 2 == 0):
            out += [("x", 1, 2, dz)]
        elif dx == -1 and part == "B" and dz % 2 == 1:
            out += [("x", -1, 2, dz)]
    if along_z:
        if dz == 0:
            out += [("z", 1, dx, 1), ("z", -1, dx, -1)]
        elif 0 < dz < 3 or (dz == 3 and (part == "B" or dx in (0, 1))):
            out += [("z", 1, dx, dz + 1)]
        elif -3 < dz < 0 or (dz == -3 and part == "A" and dx in (2, -1)):
            out += [("z", -1, dx, dz - 1 if dz > -3 else 4)]
    return out


def rel(dx, dz):
    return (dx % NX) * NZ + dz % NZ


class Gather:
    def __init__(self, panel, cols, rows, first_sem, arrive_sem, send_sem, recv_sem, row_send, row_recv, own_sem):
        self.panel, self.cols, self.rows = panel, cols, rows
        self.first_sem, self.arrive_sem = first_sem, arrive_sem
        self.send_sem, self.recv_sem = send_sem, recv_sem
        self.row_send, self.row_recv, self.own_sem = row_send, row_recv, own_sem
        self.row, self.col = lax.axis_index("row"), lax.axis_index("col")
        self.x, self.z = self.row // NZ, self.row % NZ
        self.y, self.k = self.col // 2, self.col % 2
        x, y, z, k = self.x, self.y, self.z, self.k
        self.to_row = ((x + y) % NX) * NZ + (2 * (z % 4) + k + 6 + 4 * (z // 4)) % NZ
        self.to_col = 2 * x + z // 4
        self.to_slot = (z % 4) * NC + self.col
        u = (z + 10 - 4 * k) % NZ
        self.from_row = y * NZ + 4 * k + u // 2
        self.from_col = ((x + NX - y) % NX) * 2 + u % 2
        self.stays = (self.to_row == self.row) & (self.to_col == self.col)
        self.moves = jnp.logical_not(self.stays)
        self.home = self.slot(0, 0)
        self.sent = []

    def slot(self, dx, dz):
        xh = (self.x - dx + 2 * NX) % NX
        u = (self.z - dz + 2 * NZ + 10 - 4 * self.k) % NZ
        return (u // 2) * NC + ((xh + NX - self.y) % NX) * 2 + u % 2

    def neighbour(self, axis, step):
        if axis == "x":
            return (((self.x + step + NX) % NX) * NZ + self.z, self.col)
        return (self.x * NZ + (self.z + step + NZ) % NZ, self.col)

    def peer(self, i):
        return (self.row, (self.col + i) % NC)

    def barrier(self):
        sem = pltpu.get_barrier_semaphore()
        near = [self.neighbour(a, s) for a in "xz" for s in (1, -1)]
        near += [self.peer(i) for i in range(1, NC)]
        for d in near:
            pl.semaphore_signal(sem, inc=1, device_id=d, device_id_type=MESH)

        @pl.when(self.moves)
        def _():
            for d in ((self.to_row, self.to_col), (self.from_row, self.from_col)):
                pl.semaphore_signal(sem, inc=1, device_id=d, device_id_type=MESH)
            pl.semaphore_wait(sem, len(near) + 2)

        pl.when(self.stays)(lambda: pl.semaphore_wait(sem, len(near)))

    def first(self, slot):
        return pltpu.make_async_remote_copy(
            self.panel, self.cols.at[:, slot], self.first_sem, self.arrive_sem,
            device_id=(self.to_row, self.to_col), device_id_type=MESH,
        )

    def first_stays(self):
        return pltpu.make_async_copy(self.panel, self.cols.at[:, self.home], self.first_sem)

    def row_copy(self, i, col):
        return pltpu.make_async_remote_copy(
            self.panel, self.rows.at[:, col], self.row_send.at[i], self.row_recv.at[i],
            device_id=self.peer(i + 1), device_id_type=MESH,
        )

    def row_own(self):
        return pltpu.make_async_copy(self.panel, self.rows.at[:, self.col], self.own_sem)

    def start(self):
        pl.when(self.moves)(lambda: self.first(self.to_slot).start())
        pl.when(self.stays)(lambda: self.first_stays().start())
        for i in range(NC - 1):
            self.row_copy(i, self.col).start()
        self.row_own().start()

    def piece(self, part, slot):
        return self.cols.at[:, slot, pl.ds(*PART[part])]

    def move(self, part, slot, i, dx, dz, to):
        ref = self.piece(part, slot)
        return pltpu.make_async_remote_copy(
            ref, ref, self.send_sem.at[i], self.recv_sem.at[0 if part == "A" else 1, rel(dx, dz)],
            device_id=to, device_id_type=MESH,
        )

    def arrival(self, part, dx, dz):
        slot = self.slot(dx, dz)
        if (dx, dz) != (0, 0):
            self.move(part, slot, 0, dx, dz, self.neighbour("x", 1)).wait_recv()
        elif part == "A":
            pl.when(self.moves)(lambda: self.first(self.home).wait_recv())
            pl.when(self.stays)(lambda: self.first_stays().wait())
        for axis, step, ndx, ndz in onward(part, dx, dz):
            self.move(part, slot, len(self.sent), ndx, ndz, self.neighbour(axis, step)).start()
            self.sent.append(part)

    def point(self, h):
        for part, dx, dz in PLAN.get(h, ()):
            self.arrival(part, dx, dz)

    def wait_rows(self):
        for i in range(NC - 1):
            self.row_copy(i, (self.col + NC - 1 - i) % NC).wait_recv()
        self.row_own().wait()

    def drain(self):
        for i, part in enumerate(self.sent):
            self.move(part, self.home, i, 0, 0, self.neighbour("x", 1)).wait_send()
        pl.when(self.moves)(lambda: self.first(self.to_slot).wait_send())
        for i in range(NC - 1):
            self.row_copy(i, self.col).wait_send()


DMA = pltpu.SemaphoreType.DMA
GATHER_SEMS = [DMA, DMA, DMA((62,)), DMA((2, NX * NZ)), DMA((NC - 1,)), DMA((NC - 1,)), DMA]


def dot(a, b, ca, cb, precision=None):
    return lax.dot_general(
        a, b, (((ca,), (cb,)), ((), ())), precision=precision, preferred_element_type=F32
    )


def split3(x):
    hi = x.astype(BF)
    rest = x - hi.astype(F32)
    mid = rest.astype(BF)
    return hi, mid, (rest - mid.astype(F32)).astype(BF)


def stack6(x, axis, left):
    h, m, l = split3(x)
    return jnp.concatenate([h, h, m, h, l, m] if left else [h, m, h, l, h, m], axis=axis)


def spread(x, k):
    return jnp.broadcast_to(x[k : k + 1, :], (8, 128))


def base(x, point):
    lane = lax.broadcasted_iota(jnp.int32, (8, 128), 1)
    sub = lax.broadcasted_iota(jnp.int32, (8, 128), 0)
    half = jnp.where(lane < 64, 0, 64)
    x = list(x)
    e = [jnp.where(lane - half == sub + 8 * g, 1.0, 0.0).astype(F32) for g in range(8)]
    out = []
    for p in range(8):
        point(p)
        t = {
            g: [
                jnp.take_along_axis(x[g], half + (8 * p + c), axis=1, mode="promise_in_bounds")
                for c in range(8)
            ]
            for g in range(p, 8)
        }
        pivots = t[p][0]
        for k in range(8):
            d = spread(t[p][k], k)
            pivots = jnp.where(sub == k, d, pivots)
            r = 1.0 / d
            pe, px = spread(e[p], k), spread(x[p], k)
            top = {c: spread(t[p][c], k) for c in range(k + 1, 8)}
            for g in range(p, 8):
                if g == p and k == 7:
                    continue
                m = t[g][k] * r
                if g == p:
                    m = jnp.where(sub > k, m, 0.0)
                for c in range(k + 1, 8):
                    t[g][c] = t[g][c] - m * top[c]
                if p < 7:
                    x[g] = x[g] - m * px
                e[g] = e[g] - m * pe
        out.append(e[p] * lax.rsqrt(pivots))
    return jnp.concatenate(out, axis=0)


def factor(w, v, s6, point):
    lane = lax.broadcasted_iota(jnp.int32, (8, 128), 1)
    wide = lax.broadcasted_iota(jnp.int32, (64, 512), 1)
    wide2 = lax.broadcasted_iota(jnp.int32, (128, 512), 1)

    def step(t, carry):
        o = pl.multiple_of(t * 128, 128)
        for s in range(2):
            at = pl.multiple_of(o + 64 * s, 64)
            x = []
            for g in range(8):
                rows = pl.ds(pl.multiple_of(at + 8 * g, 8), 8)
                a, b = w[0, rows, pl.ds(o, 128)], w[1, rows, pl.ds(o, 128)]
                if s == 0:
                    x.append(jnp.where(lane < 64, a, pltpu.roll(b, 64, 1)))
                else:
                    x.append(jnp.where(lane < 64, pltpu.roll(a, 64, 1), b))
            y = base(x, functools.partial(point, t, s))
            here = (wide >= at) & (wide < at + 64)
            for b in range(2):
                yb = y[:, 64 * b : 64 * b + 64]
                new = dot(yb, w[b, pl.ds(at, 64), :], 1, 0, HIGHEST)
                new = jnp.where(here, jnp.concatenate([yb] * 8, axis=1), new)
                w[b, pl.ds(at, 64), :] = jnp.where(wide < at + 64, new, 0.0)
                if s == 0:
                    v[b, 0:64, :] = jnp.where((wide >= at + 64) & (wide < at + 128), 0.0, new)
                    below = w[b, pl.ds(at + 64, 64), pl.ds(o, 128)][:, 0:64]
                    lower = dot(below, yb, 1, 1, HIGHEST)
                    rest = jnp.where(here, 0.0, w[b, pl.ds(at + 64, 64), :])
                    w[b, pl.ds(at + 64, 64), :] = rest - dot(lower, new, 1, 0, HIGHEST)
                else:
                    v[b, 64:128, :] = new
        here = (wide2 >= o) & (wide2 < o + 128)

        @pl.when(t < 3)
        def _():
            for b in range(2):
                s6[b] = stack6(v[b], 0, False)

        def chunk(i, c):
            rows = pl.ds(pl.multiple_of(i * 128, 128), 128)
            for b in range(2):
                lower = v[b, :, rows].T
                rest = jnp.where(here, 0.0, w[b, rows, :])
                w[b, rows, :] = rest - dot(stack6(lower, 1, True), s6[b], 1, 0)
            return c

        lax.fori_loop(t + 1, 4, chunk, 0)
        return carry

    lax.fori_loop(0, 4, step, 0)


def solve(x, ys, b):
    half = x.shape[1] // 2
    out = []
    for lo, depth in ((0, half), (half, 2 * half)):
        acc = None
        for y in ys:
            term = dot(x[:, :depth], y[b, lo : lo + half, :depth], 1, 1)
            acc = term if acc is None else acc + term
        out.append(acc)
    return jnp.concatenate(out, axis=1)


def panel_kernel(panel, diag, trail, cols_out, rows_out, own_out, trail_out, cols, rows, w, v, s6, hi, mid, lo, full, in_sems, *sems):
    fetch = pltpu.make_async_copy(diag, w, in_sems.at[0])
    fetch.start()
    gather = Gather(panel, cols, rows, *sems)
    gather.barrier()
    gather.start()
    fetch_trail = pltpu.make_async_copy(trail, trail_out, in_sems.at[1])
    fetch_trail.start()
    fetch.wait()

    def point(t, s, p):
        for i in range(4):
            h = (2 * i + s) * 8 + p
            if h in PLAN:
                pl.when(t == i)(functools.partial(gather.point, h))

    factor(w, v, s6, point)
    ys = (hi, mid, lo)
    for b in range(2):
        hi[b], mid[b], lo[b] = split3(w[b])

    def solve_cols(group):
        slots = [gather.slot(dx, dz) for dx, dz in group]
        for b in range(2):
            x = jnp.concatenate([cols[b, i] for i in slots], axis=0)
            x = solve(x, ys, b).astype(BF)
            for n, i in enumerate(slots):
                cols_out[b, i] = x[48 * n : 48 * n + 48]

    def solve_rows():
        gather.wait_rows()
        for b in range(2):
            full[b] = solve(jnp.concatenate([rows[b, i] for i in range(NC)], axis=0), ys, b)
            for i in range(NC):
                rows_out[b, i] = full[b, 48 * i : 48 * i + 48].astype(BF)
            own_out[b] = full[b, pl.ds(pl.multiple_of(gather.col * 48, 16), 48)]

    done = [e for h in sorted(PLAN) if h < LAST for e in PLAN[h]]
    late = list(PLAN[LAST])
    ready = [e[1:] for e in done if ("A",) + e[1:] in done and e[0] == "B"]
    solve_rows()
    while late or ready:
        while late and (len(ready) < 4 or len(late) > 3 * len(ready)):
            event = late.pop(0)
            gather.arrival(*event)
            done.append(event)
            if ("A",) + event[1:] in done and ("B",) + event[1:] in done:
                ready.append(event[1:])
        solve_cols(ready[:4])
        ready = ready[4:]
    gather.drain()
    fetch_trail.wait()


def panel_step(panel, diagonal, trailing):
    nb, count, k = panel.shape
    vmem = pl.BlockSpec(memory_space=pltpu.VMEM)
    hbm = pl.BlockSpec(memory_space=pltpu.HBM)
    return pl.pallas_call(
        panel_kernel,
        in_specs=[hbm] * 3,
        out_specs=[vmem] * 4,
        out_shape=[
            jax.ShapeDtypeStruct((nb, NX * NZ, count, k), BF),
            jax.ShapeDtypeStruct((nb, NC, count, k), BF),
            jax.ShapeDtypeStruct(panel.shape, F32),
            jax.ShapeDtypeStruct(trailing.shape, F32),
        ],
        scratch_shapes=[
            pltpu.VMEM((nb, NX * NZ, count, k), BF),
            pltpu.VMEM((nb, NC, count, k), BF),
            pltpu.VMEM(diagonal.shape, F32),
            pltpu.VMEM((nb, 128, k), F32),
            pltpu.VMEM((nb, 768, k), BF),
            pltpu.VMEM(diagonal.shape, BF),
            pltpu.VMEM(diagonal.shape, BF),
            pltpu.VMEM(diagonal.shape, BF),
            pltpu.VMEM((nb, NC * count, k), F32),
            DMA((2,)),
        ] + GATHER_SEMS,
        compiler_params=pltpu.CompilerParams(
            collective_id=0, has_side_effects=True, vmem_limit_bytes=42 << 20
        ),
        cost_estimate=pl.CostEstimate(flops=10**10, bytes_accessed=10**7, transcendentals=0),
        name="panel_step",
    )(*(pltpu.with_memory_space_constraint(a, pltpu.HBM) for a in (panel, diagonal, trailing)))


WIDE = 256


def update_kernel(pat, cols, rows, own, trail, out, solved, buf, own_buf, sems, own_sem):
    row, col = lax.axis_index("row"), lax.axis_index("col")
    nb, m, n = buf.shape
    count = own.shape[1]
    first = (row * NC + col) * count
    low, high = first // BLK, (first + count - 1) // BLK
    at = first + lax.broadcasted_iota(jnp.int32, own.shape[1:], 0)
    keep = jnp.where(at < high * BLK, pat[low], pat[high]).astype(F32)
    for b in range(nb):
        own_buf[b] = own[b] * keep
    own_copy = pltpu.make_async_copy(own_buf, solved, own_sem)
    own_copy.start()
    keep_rows = [pat[row * (m // BLK) + i] for i in range(m // BLK)]
    copies = []
    for b in range(nb):
        for j in range(n // WIDE):
            there = pl.ds(j * WIDE, WIDE)
            prod = dot(rows[b], cols[b, there], 1, 1)
            for q in range(WIDE // BLK):
                keep_col = pat[col * (n // BLK) + j * (WIDE // BLK) + q]
                for i, keep_row in enumerate(keep_rows):
                    r = slice(i * BLK, (i + 1) * BLK)
                    c = slice(j * WIDE + q * BLK, j * WIDE + (q + 1) * BLK)
                    both = (keep_col * keep_row).astype(F32)
                    buf[b, r, c] = trail[b, r, c] - both * prod[r, q * BLK : (q + 1) * BLK]
            copy = pltpu.make_async_copy(buf.at[b, :, there], out.at[b, :, there], sems.at[b, j])
            copy.start()
            copies.append(copy)
    for copy in copies:
        copy.wait()
    own_copy.wait()


def update(pattern, cols, rows, own, trailing):
    vmem = pl.BlockSpec(memory_space=pltpu.VMEM)
    hbm = pl.BlockSpec(memory_space=pltpu.HBM)
    nb, m, n = trailing.shape
    return pl.pallas_call(
        update_kernel,
        in_specs=[pl.BlockSpec(memory_space=pltpu.SMEM)] + [vmem] * 4,
        out_specs=[hbm] * 2,
        out_shape=[jax.ShapeDtypeStruct(trailing.shape, F32), jax.ShapeDtypeStruct(own.shape, F32)],
        scratch_shapes=[
            pltpu.VMEM(trailing.shape, F32),
            pltpu.VMEM(own.shape, F32),
            DMA((nb, n // WIDE)),
            DMA,
        ],
        compiler_params=pltpu.CompilerParams(vmem_limit_bytes=36 << 20),
        cost_estimate=pl.CostEstimate(flops=10**9, bytes_accessed=10**7, transcendentals=0),
        name="update",
    )(pattern, cols, rows, own, trailing)


def per_device(trailing, panel, diagonal, pattern):
    cols, rows, own, trail = panel_step(panel, diagonal, trailing)
    nb, _, _, k = cols.shape
    return tuple(update(pattern, cols.reshape(nb, -1, k), rows.reshape(nb, -1, k), own, trail))


def solution(mesh):
    return jax.shard_map(
        per_device,
        mesh=mesh,
        in_specs=(P(None, "row", "col"), P(None, ("row", "col"), None), P(), P()),
        out_specs=(P(None, "row", "col"), P(None, ("row", "col"), None)),
        check_vma=False,
    )
```

```python
import functools

import jax
import jax.numpy as jnp
from jax import lax
from jax.experimental import pallas as pl
from jax.experimental.pallas import tpu as pltpu
from jax.sharding import PartitionSpec as P

BLK = 128
F32 = jnp.float32
BF = jnp.bfloat16
HIGHEST = lax.Precision.HIGHEST
MESH = pl.DeviceIdType.MESH
NX, NZ, NC = 4, 8, 8

PLAN = {
    5: [('A', 0, 0), ('B', 0, 0)],
    13: [('A', 1, 0), ('A', -1, 0), ('A', 0, 1), ('A', 0, -1)],
    15: [('B', 1, 0), ('B', -1, 0), ('B', 0, 1), ('B', 0, -1)],
    19: [('A', 2, 0)],
    24: [('A', 1, 1), ('A', -1, 1), ('A', 0, 2), ('A', 1, -1), ('A', -1, -1), ('A', 0, -2)],
    27: [('B', -1, 1), ('B', -1, -1)],
    28: [('A', 2, 1), ('A', 2, -1)],
    29: [('B', 0, 2), ('B', 0, -2)],
    31: [('B', 2, 0), ('B', 1, 1), ('B', 1, -1)],
    35: [('A', 1, 2), ('A', -1, 2), ('A', 0, 3), ('A', 1, -2), ('A', -1, -2), ('A', 0, -3)],
    38: [('A', 2, 2), ('A', 2, -2)],
    40: [('B', 0, 3), ('B', 0, -3)],
    41: [('B', 1, 2), ('B', 1, -2)],
    44: [('A', 1, -3), ('A', -1, -3), ('B', 2, 1), ('B', 2, -1)],
    45: [('A', 2, -3)],
    46: [('A', 1, 3), ('A', -1, 3), ('A', 0, 4)],
    48: [('B', -1, 2), ('B', -1, -2), ('A', 2, 3)],
    51: [('B', 0, 4), ('A', -1, 4)],
    52: [('A', 2, 4), ('A', 1, 4)],
    54: [('B', -1, 3), ('B', -1, -3)],
    59: [('B', 1, 3), ('B', 1, -3)],
    60: [('B', 2, 2), ('B', 2, -2)],
    61: [('B', -1, 4)],
    63: [('B', 1, 4)],
    64: [('B', 2, 3), ('B', 2, -3), ('B', 2, 4)],
}
LAST = 64
PART = {"A": (0, 16), "B": (16, 32)}


def onward(part, dx, dz):
    out = []
    along_x = part == "B" or dz == 0
    along_z = part == "A" or dx == 0
    if along_x:
        if dx == 0:
            out += [("x", 1, 1, dz), ("x", -1, -1, dz)]
        elif dx == 1 and (part == "A" or dz % 2 == 0):
            out += [("x", 1, 2, dz)]
        elif dx == -1 and part == "B" and dz % 2 == 1:
            out += [("x", -1, 2, dz)]
    if along_z:
        if dz == 0:
            out += [("z", 1, dx, 1), ("z", -1, dx, -1)]
        elif 0 < dz < 3 or (dz == 3 and (part == "B" or dx in (0, 1))):
            out += [("z", 1, dx, dz + 1)]
        elif -3 < dz < 0 or (dz == -3 and part == "A" and dx in (2, -1)):
            out += [("z", -1, dx, dz - 1 if dz > -3 else 4)]
    return out


def rel(dx, dz):
    return (dx % NX) * NZ + dz % NZ


class Gather:
    def __init__(self, panel, cols, rows, first_sem, arrive_sem, send_sem, recv_sem, row_send, row_recv, own_sem):
        self.panel, self.cols, self.rows = panel, cols, rows
        self.first_sem, self.arrive_sem = first_sem, arrive_sem
        self.send_sem, self.recv_sem = send_sem, recv_sem
        self.row_send, self.row_recv, self.own_sem = row_send, row_recv, own_sem
        self.row, self.col = lax.axis_index("row"), lax.axis_index("col")
        self.x, self.z = self.row // NZ, self.row % NZ
        self.y, self.k = self.col // 2, self.col % 2
        x, y, z, k = self.x, self.y, self.z, self.k
        self.to_row = ((x + y) % NX) * NZ + (2 * (z % 4) + k + 6 + 4 * (z // 4)) % NZ
        self.to_col = 2 * x + z // 4
        self.to_slot = (z % 4) * NC + self.col
        u = (z + 10 - 4 * k) % NZ
        self.from_row = y * NZ + 4 * k + u // 2
        self.from_col = ((x + NX - y) % NX) * 2 + u % 2
        self.stays = (self.to_row == self.row) & (self.to_col == self.col)
        self.moves = jnp.logical_not(self.stays)
        self.home = self.slot(0, 0)
        self.sent = []

    def slot(self, dx, dz):
        xh = (self.x - dx + 2 * NX) % NX
        u = (self.z - dz + 2 * NZ + 10 - 4 * self.k) % NZ
        return (u // 2) * NC + ((xh + NX - self.y) % NX) * 2 + u % 2

    def neighbour(self, axis, step):
        if axis == "x":
            return (((self.x + step + NX) % NX) * NZ + self.z, self.col)
        return (self.x * NZ + (self.z + step + NZ) % NZ, self.col)

    def peer(self, i):
        return (self.row, (self.col + i) % NC)

    def barrier(self):
        sem = pltpu.get_barrier_semaphore()
        near = [self.neighbour(a, s) for a in "xz" for s in (1, -1)]
        near += [self.peer(i) for i in range(1, NC)]
        for d in near:
            pl.semaphore_signal(sem, inc=1, device_id=d, device_id_type=MESH)

        @pl.when(self.moves)
        def _():
            for d in ((self.to_row, self.to_col), (self.from_row, self.from_col)):
                pl.semaphore_signal(sem, inc=1, device_id=d, device_id_type=MESH)
            pl.semaphore_wait(sem, len(near) + 2)

        pl.when(self.stays)(lambda: pl.semaphore_wait(sem, len(near)))

    def first(self, slot):
        return pltpu.make_async_remote_copy(
            self.panel, self.cols.at[:, slot], self.first_sem, self.arrive_sem,
            device_id=(self.to_row, self.to_col), device_id_type=MESH,
        )

    def first_stays(self):
        return pltpu.make_async_copy(self.panel, self.cols.at[:, self.home], self.first_sem)

    def row_copy(self, i, col):
        return pltpu.make_async_remote_copy(
            self.panel, self.rows.at[:, col], self.row_send.at[i], self.row_recv.at[i],
            device_id=self.peer(i + 1), device_id_type=MESH,
        )

    def row_own(self):
        return pltpu.make_async_copy(self.panel, self.rows.at[:, self.col], self.own_sem)

    def start(self):
        pl.when(self.moves)(lambda: self.first(self.to_slot).start())
        pl.when(self.stays)(lambda: self.first_stays().start())
        for i in range(NC - 1):
            self.row_copy(i, self.col).start()
        self.row_own().start()

    def piece(self, part, slot):
        return self.cols.at[:, slot, pl.ds(*PART[part])]

    def move(self, part, slot, i, dx, dz, to):
        ref = self.piece(part, slot)
        return pltpu.make_async_remote_copy(
            ref, ref, self.send_sem.at[i], self.recv_sem.at[0 if part == "A" else 1, rel(dx, dz)],
            device_id=to, device_id_type=MESH,
        )

    def arrival(self, part, dx, dz):
        slot = self.slot(dx, dz)
        if (dx, dz) != (0, 0):
            self.move(part, slot, 0, dx, dz, self.neighbour("x", 1)).wait_recv()
        elif part == "A":
            pl.when(self.moves)(lambda: self.first(self.home).wait_recv())
            pl.when(self.stays)(lambda: self.first_stays().wait())
        for axis, step, ndx, ndz in onward(part, dx, dz):
            self.move(part, slot, len(self.sent), ndx, ndz, self.neighbour(axis, step)).start()
            self.sent.append(part)

    def point(self, h):
        for part, dx, dz in PLAN.get(h, ()):
            self.arrival(part, dx, dz)

    def wait_rows(self):
        for i in range(NC - 1):
            self.row_copy(i, (self.col + NC - 1 - i) % NC).wait_recv()
        self.row_own().wait()

    def drain(self):
        for i, part in enumerate(self.sent):
            self.move(part, self.home, i, 0, 0, self.neighbour("x", 1)).wait_send()
        pl.when(self.moves)(lambda: self.first(self.to_slot).wait_send())
        for i in range(NC - 1):
            self.row_copy(i, self.col).wait_send()


DMA = pltpu.SemaphoreType.DMA
GATHER_SEMS = [DMA, DMA, DMA((62,)), DMA((2, NX * NZ)), DMA((NC - 1,)), DMA((NC - 1,)), DMA]


def dot(a, b, ca, cb, precision=None):
    return lax.dot_general(
        a, b, (((ca,), (cb,)), ((), ())), precision=precision, preferred_element_type=F32
    )


def split3(x):
    hi = x.astype(BF)
    rest = x - hi.astype(F32)
    mid = rest.astype(BF)
    return hi, mid, (rest - mid.astype(F32)).astype(BF)


def stack6(x, axis, left):
    h, m, l = split3(x)
    return jnp.concatenate([h, h, m, h, l, m] if left else [h, m, h, l, h, m], axis=axis)


def spread(x, k):
    return jnp.broadcast_to(x[k : k + 1, :], (8, 128))


def base(x, point):
    lane = lax.broadcasted_iota(jnp.int32, (8, 128), 1)
    sub = lax.broadcasted_iota(jnp.int32, (8, 128), 0)
    half = jnp.where(lane < 64, 0, 64)
    x = list(x)
    e = [jnp.where(lane - half == sub + 8 * g, 1.0, 0.0).astype(F32) for g in range(8)]
    out = []
    for p in range(8):
        point(p)
        t = {
            g: [
                jnp.take_along_axis(x[g], half + (8 * p + c), axis=1, mode="promise_in_bounds")
                for c in range(8)
            ]
            for g in range(p, 8)
        }
        pivots = t[p][0]
        for k in range(8):
            d = spread(t[p][k], k)
            pivots = jnp.where(sub == k, d, pivots)
            r = 1.0 / d
            pe, px = spread(e[p], k), spread(x[p], k)
            top = {c: spread(t[p][c], k) for c in range(k + 1, 8)}
            for g in range(p, 8):
                if g == p and k == 7:
                    continue
                m = t[g][k] * r
                if g == p:
                    m = jnp.where(sub > k, m, 0.0)
                for c in range(k + 1, 8):
                    t[g][c] = t[g][c] - m * top[c]
                if p < 7:
                    x[g] = x[g] - m * px
                e[g] = e[g] - m * pe
        out.append(e[p] * lax.rsqrt(pivots))
    return jnp.concatenate(out, axis=0)


def factor(w, v, s6, point):
    lane = lax.broadcasted_iota(jnp.int32, (8, 128), 1)
    wide = lax.broadcasted_iota(jnp.int32, (64, 512), 1)
    wide2 = lax.broadcasted_iota(jnp.int32, (128, 512), 1)
    band = lax.broadcasted_iota(jnp.int32, (128, 128), 0) // 64
    same = band == lax.broadcasted_iota(jnp.int32, (128, 128), 1) // 64

    for t in range(4):
        o = t * 128
        for s in range(2):
            at = o + 64 * s
            x = []
            for g in range(8):
                rows = pl.ds(at + 8 * g, 8)
                a, b = w[0, rows, pl.ds(o, 128)], w[1, rows, pl.ds(o, 128)]
                if s == 0:
                    x.append(jnp.where(lane < 64, a, pltpu.roll(b, 64, 1)))
                else:
                    x.append(jnp.where(lane < 64, pltpu.roll(a, 64, 1), b))
            y = base(x, functools.partial(point, t, s))
            both = jnp.concatenate([w[0, pl.ds(at, 64), :], w[1, pl.ds(at, 64), :]], axis=0)
            ys = jnp.where(same, jnp.concatenate([y, y], axis=0), 0.0)
            new = dot(stack6(ys, 1, True), stack6(both, 0, False), 1, 0)
            here = (wide2 >= at) & (wide2 < at + 64)
            yt = jnp.where(same, ys, pltpu.roll(ys, 64, 1))
            yt = jnp.concatenate([yt] * 4, axis=1)
            new = jnp.where(here, yt, new)
            for b in range(2):
                part = new[64 * b : 64 * b + 64]
                w[b, pl.ds(at, 64), :] = jnp.where(wide < at + 64, part, 0.0)
                if s == 0:
                    part = jnp.where((wide >= at + 64) & (wide < at + 128), 0.0, part)
                v[b, 64 * s : 64 * s + 64, :] = part
            if s == 0:
                below = [w[b, pl.ds(at + 64, 64), pl.ds(o, 128)] for b in range(2)]
                below = jnp.concatenate([below[0], pltpu.roll(below[1], 64, 1)], axis=0)
                below = jnp.where(same, below, 0.0)
                lower = dot(stack6(below, 1, True), stack6(jnp.concatenate([y, y], axis=0), 1, False), 1, 1)
                lower = jnp.where(same, lower, 0.0)
                rest = [w[b, pl.ds(at + 64, 64), :] for b in range(2)]
                rest = jnp.where(here, 0.0, jnp.concatenate(rest, axis=0))
                rest = rest - dot(stack6(lower, 1, True), stack6(new, 0, False), 1, 0)
                for b in range(2):
                    w[b, pl.ds(at + 64, 64), :] = rest[64 * b : 64 * b + 64]
        here = (wide2 >= o) & (wide2 < o + 128)

        if t < 3:
            for b in range(2):
                s6[b] = stack6(v[b], 0, False)

        for i in range(t + 1, 4):
            rows = pl.ds(i * 128, 128)
            for b in range(2):
                lower = v[b, :, rows].T
                rest = jnp.where(here, 0.0, w[b, rows, :])
                w[b, rows, :] = rest - dot(stack6(lower, 1, True), s6[b], 1, 0)


def solve(x, ys, b):
    half = x.shape[1] // 2
    out = []
    for lo, depth in ((0, half), (half, 2 * half)):
        acc = None
        for y in ys:
            term = dot(x[:, :depth], y[b, lo : lo + half, :depth], 1, 1)
            acc = term if acc is None else acc + term
        out.append(acc)
    return jnp.concatenate(out, axis=1)


def panel_kernel(panel, diag, trail, cols_out, rows_out, own_out, trail_out, cols, rows, w, v, s6, hi, mid, lo, full, in_sems, *sems):
    fetch = pltpu.make_async_copy(diag, w, in_sems.at[0])
    fetch.start()
    gather = Gather(panel, cols, rows, *sems)
    gather.barrier()
    gather.start()
    fetch_trail = pltpu.make_async_copy(trail, trail_out, in_sems.at[1])
    fetch_trail.start()
    fetch.wait()

    def point(t, s, p):
        gather.point((2 * t + s) * 8 + p)

    factor(w, v, s6, point)
    ys = (hi, mid, lo)
    for b in range(2):
        hi[b], mid[b], lo[b] = split3(w[b])

    def solve_cols(group):
        slots = [gather.slot(dx, dz) for dx, dz in group]
        for b in range(2):
            x = jnp.concatenate([cols[b, i] for i in slots], axis=0)
            x = solve(x, ys, b).astype(BF)
            for n, i in enumerate(slots):
                cols_out[b, i] = x[48 * n : 48 * n + 48]

    def solve_rows():
        gather.wait_rows()
        for b in range(2):
            full[b] = solve(jnp.concatenate([rows[b, i] for i in range(NC)], axis=0), ys, b)
            for i in range(NC):
                rows_out[b, i] = full[b, 48 * i : 48 * i + 48].astype(BF)
            own_out[b] = full[b, pl.ds(pl.multiple_of(gather.col * 48, 16), 48)]

    done = [e for h in sorted(PLAN) if h < LAST for e in PLAN[h]]
    late = list(PLAN[LAST])
    ready = [e[1:] for e in done if ("A",) + e[1:] in done and e[0] == "B"]
    solve_rows()
    while late or ready:
        while late and (len(ready) < 4 or len(late) > 3 * len(ready)):
            event = late.pop(0)
            gather.arrival(*event)
            done.append(event)
            if ("A",) + event[1:] in done and ("B",) + event[1:] in done:
                ready.append(event[1:])
        solve_cols(ready[:4])
        ready = ready[4:]
    gather.drain()
    fetch_trail.wait()


def panel_step(panel, diagonal, trailing):
    nb, count, k = panel.shape
    vmem = pl.BlockSpec(memory_space=pltpu.VMEM)
    hbm = pl.BlockSpec(memory_space=pltpu.HBM)
    return pl.pallas_call(
        panel_kernel,
        in_specs=[hbm] * 3,
        out_specs=[vmem] * 4,
        out_shape=[
            jax.ShapeDtypeStruct((nb, NX * NZ, count, k), BF),
            jax.ShapeDtypeStruct((nb, NC, count, k), BF),
            jax.ShapeDtypeStruct(panel.shape, F32),
            jax.ShapeDtypeStruct(trailing.shape, F32),
        ],
        scratch_shapes=[
            pltpu.VMEM((nb, NX * NZ, count, k), BF),
            pltpu.VMEM((nb, NC, count, k), BF),
            pltpu.VMEM(diagonal.shape, F32),
            pltpu.VMEM((nb, 128, k), F32),
            pltpu.VMEM((nb, 768, k), BF),
            pltpu.VMEM(diagonal.shape, BF),
            pltpu.VMEM(diagonal.shape, BF),
            pltpu.VMEM(diagonal.shape, BF),
            pltpu.VMEM((nb, NC * count, k), F32),
            DMA((2,)),
        ] + GATHER_SEMS,
        compiler_params=pltpu.CompilerParams(
            collective_id=0, has_side_effects=True, vmem_limit_bytes=42 << 20
        ),
        cost_estimate=pl.CostEstimate(flops=10**10, bytes_accessed=10**7, transcendentals=0),
        name="panel_step",
    )(*(pltpu.with_memory_space_constraint(a, pltpu.HBM) for a in (panel, diagonal, trailing)))


WIDE = 256


def update_kernel(pat, cols, rows, own, trail, out, solved, buf, own_buf, sems, own_sem):
    row, col = lax.axis_index("row"), lax.axis_index("col")
    nb, m, n = buf.shape
    count = own.shape[1]
    first = (row * NC + col) * count
    low, high = first // BLK, (first + count - 1) // BLK
    at = first + lax.broadcasted_iota(jnp.int32, own.shape[1:], 0)
    keep = jnp.where(at < high * BLK, pat[low], pat[high]).astype(F32)
    for b in range(nb):
        own_buf[b] = own[b] * keep
    own_copy = pltpu.make_async_copy(own_buf, solved, own_sem)
    own_copy.start()
    keep_rows = [pat[row * (m // BLK) + i] for i in range(m // BLK)]
    copies = []
    for b in range(nb):
        for j in range(n // WIDE):
            there = pl.ds(j * WIDE, WIDE)
            prod = dot(rows[b], cols[b, there], 1, 1)
            for q in range(WIDE // BLK):
                keep_col = pat[col * (n // BLK) + j * (WIDE // BLK) + q]
                for i, keep_row in enumerate(keep_rows):
                    r = slice(i * BLK, (i + 1) * BLK)
                    c = slice(j * WIDE + q * BLK, j * WIDE + (q + 1) * BLK)
                    both = (keep_col * keep_row).astype(F32)
                    buf[b, r, c] = trail[b, r, c] - both * prod[r, q * BLK : (q + 1) * BLK]
            copy = pltpu.make_async_copy(buf.at[b, :, there], out.at[b, :, there], sems.at[b, j])
            copy.start()
            copies.append(copy)
    for copy in copies:
        copy.wait()
    own_copy.wait()


def update(pattern, cols, rows, own, trailing):
    vmem = pl.BlockSpec(memory_space=pltpu.VMEM)
    hbm = pl.BlockSpec(memory_space=pltpu.HBM)
    nb, m, n = trailing.shape
    return pl.pallas_call(
        update_kernel,
        in_specs=[pl.BlockSpec(memory_space=pltpu.SMEM)] + [vmem] * 4,
        out_specs=[hbm] * 2,
        out_shape=[jax.ShapeDtypeStruct(trailing.shape, F32), jax.ShapeDtypeStruct(own.shape, F32)],
        scratch_shapes=[
            pltpu.VMEM(trailing.shape, F32),
            pltpu.VMEM(own.shape, F32),
            DMA((nb, n // WIDE)),
            DMA,
        ],
        compiler_params=pltpu.CompilerParams(vmem_limit_bytes=36 << 20),
        cost_estimate=pl.CostEstimate(flops=10**9, bytes_accessed=10**7, transcendentals=0),
        name="update",
    )(pattern, cols, rows, own, trailing)


def per_device(trailing, panel, diagonal, pattern):
    cols, rows, own, trail = panel_step(panel, diagonal, trailing)
    nb, _, _, k = cols.shape
    return tuple(update(pattern, cols.reshape(nb, -1, k), rows.reshape(nb, -1, k), own, trail))


def solution(mesh):
    return jax.shard_map(
        per_device,
        mesh=mesh,
        in_specs=(P(None, "row", "col"), P(None, ("row", "col"), None), P(), P()),
        out_specs=(P(None, "row", "col"), P(None, ("row", "col"), None)),
        check_vma=False,
    )
```

```python
import functools

import jax
import jax.numpy as jnp
from jax import lax
from jax.experimental import pallas as pl
from jax.experimental.pallas import tpu as pltpu
from jax.sharding import PartitionSpec as P

BLK = 128
F32 = jnp.float32
BF = jnp.bfloat16
HIGHEST = lax.Precision.HIGHEST
MESH = pl.DeviceIdType.MESH
NX, NZ, NC = 4, 8, 8

PLAN = {
    3: [('A', 0, 0)],
    5: [('B', 0, 0)],
    10: [('A', 1, 0), ('A', -1, 0), ('A', 0, 1), ('A', 0, -1)],
    14: [('B', 1, 0), ('B', -1, 0), ('B', 0, 1), ('B', 0, -1)],
    17: [('A', 2, 0)],
    22: [('A', 1, 1), ('A', -1, 1), ('A', 0, 2), ('A', 1, -1), ('A', -1, -1), ('A', 0, -2)],
    26: [('A', 2, 1), ('A', 2, -1)],
    27: [('B', 0, 2), ('B', 0, -2), ('B', -1, 1), ('B', -1, -1)],
    31: [('B', 2, 0), ('B', 1, 1), ('B', 1, -1)],
    34: [('A', 1, 2), ('A', -1, 2), ('A', 0, 3), ('A', 1, -2), ('A', -1, -2), ('A', 0, -3)],
    37: [('A', 2, 2), ('A', 2, -2)],
    39: [('B', 0, 3), ('B', 0, -3)],
    40: [('B', 1, 2), ('B', 1, -2)],
    44: [('A', 1, -3), ('A', -1, -3)],
    45: [('A', 2, -3)],
    46: [('A', 1, 3), ('A', -1, 3), ('A', 0, 4)],
    48: [('A', 2, 3)],
    49: [('B', -1, 2), ('B', -1, -2), ('B', 2, 1), ('B', 2, -1)],
    51: [('B', 0, 4)],
    52: [('A', -1, 4)],
    53: [('A', 2, 4), ('A', 1, 4)],
    55: [('B', -1, 3), ('B', -1, -3)],
    59: [('B', 1, 3), ('B', 1, -3)],
    60: [('B', 2, 2), ('B', 2, -2), ('B', -1, 4)],
    63: [('B', 1, 4)],
    64: [('B', 2, 3), ('B', 2, -3), ('B', 2, 4)],
}
LAST = 64
PART = {"A": (0, 16), "B": (16, 32)}


def onward(part, dx, dz):
    out = []
    along_x = part == "B" or dz == 0
    along_z = part == "A" or dx == 0
    if along_x:
        if dx == 0:
            out += [("x", 1, 1, dz), ("x", -1, -1, dz)]
        elif dx == 1 and (part == "A" or dz % 2 == 0):
            out += [("x", 1, 2, dz)]
        elif dx == -1 and part == "B" and dz % 2 == 1:
            out += [("x", -1, 2, dz)]
    if along_z:
        if dz == 0:
            out += [("z", 1, dx, 1), ("z", -1, dx, -1)]
        elif 0 < dz < 3 or (dz == 3 and (part == "B" or dx in (0, 1))):
            out += [("z", 1, dx, dz + 1)]
        elif -3 < dz < 0 or (dz == -3 and part == "A" and dx in (2, -1)):
            out += [("z", -1, dx, dz - 1 if dz > -3 else 4)]
    return out


def rel(dx, dz):
    return (dx % NX) * NZ + dz % NZ


class Gather:
    def __init__(self, panel, cols, rows, first_sem, arrive_sem, send_sem, recv_sem, row_send, row_recv, own_sem):
        self.panel, self.cols, self.rows = panel, cols, rows
        self.first_sem, self.arrive_sem = first_sem, arrive_sem
        self.send_sem, self.recv_sem = send_sem, recv_sem
        self.row_send, self.row_recv, self.own_sem = row_send, row_recv, own_sem
        self.row, self.col = lax.axis_index("row"), lax.axis_index("col")
        self.x, self.z = self.row // NZ, self.row % NZ
        self.y, self.k = self.col // 2, self.col % 2
        x, y, z, k = self.x, self.y, self.z, self.k
        self.to_row = ((x + y) % NX) * NZ + (2 * (z % 4) + k + 6 + 4 * (z // 4)) % NZ
        self.to_col = 2 * x + z // 4
        self.to_slot = (z % 4) * NC + self.col
        u = (z + 10 - 4 * k) % NZ
        self.from_row = y * NZ + 4 * k + u // 2
        self.from_col = ((x + NX - y) % NX) * 2 + u % 2
        self.stays = (self.to_row == self.row) & (self.to_col == self.col)
        self.moves = jnp.logical_not(self.stays)
        self.home = self.slot(0, 0)
        self.sent = []

    def slot(self, dx, dz):
        xh = (self.x - dx + 2 * NX) % NX
        u = (self.z - dz + 2 * NZ + 10 - 4 * self.k) % NZ
        return (u // 2) * NC + ((xh + NX - self.y) % NX) * 2 + u % 2

    def neighbour(self, axis, step):
        if axis == "x":
            return (((self.x + step + NX) % NX) * NZ + self.z, self.col)
        return (self.x * NZ + (self.z + step + NZ) % NZ, self.col)

    def peer(self, i):
        return (self.row, (self.col + i) % NC)

    def barrier(self):
        sem = pltpu.get_barrier_semaphore()
        near = [self.neighbour(a, s) for a in "xz" for s in (1, -1)]
        near += [self.peer(i) for i in range(1, NC)]
        for d in near:
            pl.semaphore_signal(sem, inc=1, device_id=d, device_id_type=MESH)

        @pl.when(self.moves)
        def _():
            for d in ((self.to_row, self.to_col), (self.from_row, self.from_col)):
                pl.semaphore_signal(sem, inc=1, device_id=d, device_id_type=MESH)
            pl.semaphore_wait(sem, len(near) + 2)

        pl.when(self.stays)(lambda: pl.semaphore_wait(sem, len(near)))

    def first(self, part, slot):
        i = 0 if part == "A" else 1
        return pltpu.make_async_remote_copy(
            self.panel.at[:, pl.ds(*PART[part])], self.piece(part, slot),
            self.first_sem.at[i], self.arrive_sem.at[i],
            device_id=(self.to_row, self.to_col), device_id_type=MESH,
        )

    def first_stays(self, part):
        return pltpu.make_async_copy(
            self.panel.at[:, pl.ds(*PART[part])], self.piece(part, self.home),
            self.first_sem.at[0 if part == "A" else 1],
        )

    def row_copy(self, i, col):
        return pltpu.make_async_remote_copy(
            self.panel, self.rows.at[:, col], self.row_send.at[i], self.row_recv.at[i],
            device_id=self.peer(i + 1), device_id_type=MESH,
        )

    def row_own(self):
        return pltpu.make_async_copy(self.panel, self.rows.at[:, self.col], self.own_sem)

    def start(self):
        for part in PART:
            pl.when(self.moves)(lambda: self.first(part, self.to_slot).start())
            pl.when(self.stays)(lambda: self.first_stays(part).start())
        for i in range(NC - 1):
            self.row_copy(i, self.col).start()
        self.row_own().start()

    def piece(self, part, slot):
        return self.cols.at[:, slot, pl.ds(*PART[part])]

    def move(self, part, slot, i, dx, dz, to):
        ref = self.piece(part, slot)
        return pltpu.make_async_remote_copy(
            ref, ref, self.send_sem.at[i], self.recv_sem.at[0 if part == "A" else 1, rel(dx, dz)],
            device_id=to, device_id_type=MESH,
        )

    def arrival(self, part, dx, dz):
        slot = self.slot(dx, dz)
        if (dx, dz) != (0, 0):
            self.move(part, slot, 0, dx, dz, self.neighbour("x", 1)).wait_recv()
        else:
            pl.when(self.moves)(lambda: self.first(part, self.home).wait_recv())
            pl.when(self.stays)(lambda: self.first_stays(part).wait())
        for axis, step, ndx, ndz in onward(part, dx, dz):
            self.move(part, slot, len(self.sent), ndx, ndz, self.neighbour(axis, step)).start()
            self.sent.append(part)

    def point(self, h):
        for part, dx, dz in PLAN.get(h, ()):
            self.arrival(part, dx, dz)

    def wait_rows(self):
        for i in range(NC - 1):
            self.row_copy(i, (self.col + NC - 1 - i) % NC).wait_recv()
        self.row_own().wait()

    def drain(self):
        for i, part in enumerate(self.sent):
            self.move(part, self.home, i, 0, 0, self.neighbour("x", 1)).wait_send()
        for part in PART:
            pl.when(self.moves)(lambda: self.first(part, self.to_slot).wait_send())
        for i in range(NC - 1):
            self.row_copy(i, self.col).wait_send()


DMA = pltpu.SemaphoreType.DMA
GATHER_SEMS = [DMA((2,)), DMA((2,)), DMA((62,)), DMA((2, NX * NZ)), DMA((NC - 1,)), DMA((NC - 1,)), DMA]


def dot(a, b, ca, cb, precision=None):
    return lax.dot_general(
        a, b, (((ca,), (cb,)), ((), ())), precision=precision, preferred_element_type=F32
    )


def split3(x):
    hi = x.astype(BF)
    rest = x - hi.astype(F32)
    mid = rest.astype(BF)
    return hi, mid, (rest - mid.astype(F32)).astype(BF)


def stack6(x, axis, left):
    h, m, l = split3(x)
    return jnp.concatenate([h, h, m, h, l, m] if left else [h, m, h, l, h, m], axis=axis)


def spread(x, k):
    return jnp.broadcast_to(x[k : k + 1, :], (8, 128))


def base(x, point):
    lane = lax.broadcasted_iota(jnp.int32, (8, 128), 1)
    sub = lax.broadcasted_iota(jnp.int32, (8, 128), 0)
    half = jnp.where(lane < 64, 0, 64)
    x = list(x)
    e = [jnp.where(lane - half == sub + 8 * g, 1.0, 0.0).astype(F32) for g in range(8)]
    out = []
    for p in range(8):
        point(p)
        t = {
            g: [
                jnp.take_along_axis(x[g], half + (8 * p + c), axis=1, mode="promise_in_bounds")
                for c in range(8)
            ]
            for g in range(p, 8)
        }
        pivots = t[p][0]
        for k in range(8):
            d = spread(t[p][k], k)
            pivots = jnp.where(sub == k, d, pivots)
            r = 1.0 / d
            pe, px = spread(e[p], k), spread(x[p], k)
            top = {c: spread(t[p][c], k) for c in range(k + 1, 8)}
            for g in range(p, 8):
                if g == p and k == 7:
                    continue
                m = t[g][k] * r
                if g == p:
                    m = jnp.where(sub > k, m, 0.0)
                for c in range(k + 1, 8):
                    t[g][c] = t[g][c] - m * top[c]
                if p < 7:
                    x[g] = x[g] - m * px
                e[g] = e[g] - m * pe
        out.append(e[p] * lax.rsqrt(pivots))
    return jnp.concatenate(out, axis=0)


def factor(w, v, s6, point):
    lane = lax.broadcasted_iota(jnp.int32, (8, 128), 1)
    wide = lax.broadcasted_iota(jnp.int32, (64, 512), 1)
    wide2 = lax.broadcasted_iota(jnp.int32, (128, 512), 1)
    band = lax.broadcasted_iota(jnp.int32, (128, 128), 0) // 64
    same = band == lax.broadcasted_iota(jnp.int32, (128, 128), 1) // 64

    for t in range(4):
        o = t * 128
        for s in range(2):
            at = o + 64 * s
            x = []
            for g in range(8):
                rows = pl.ds(at + 8 * g, 8)
                a, b = w[0, rows, pl.ds(o, 128)], w[1, rows, pl.ds(o, 128)]
                if s == 0:
                    x.append(jnp.where(lane < 64, a, pltpu.roll(b, 64, 1)))
                else:
                    x.append(jnp.where(lane < 64, pltpu.roll(a, 64, 1), b))
            y = base(x, functools.partial(point, t, s))
            both = jnp.concatenate([w[0, pl.ds(at, 64), :], w[1, pl.ds(at, 64), :]], axis=0)
            ys = jnp.where(same, jnp.concatenate([y, y], axis=0), 0.0)
            new = dot(stack6(ys, 1, True), stack6(both, 0, False), 1, 0)
            here = (wide2 >= at) & (wide2 < at + 64)
            yt = jnp.where(same, ys, pltpu.roll(ys, 64, 1))
            yt = jnp.concatenate([yt] * 4, axis=1)
            new = jnp.where(here, yt, new)
            for b in range(2):
                part = new[64 * b : 64 * b + 64]
                w[b, pl.ds(at, 64), :] = jnp.where(wide < at + 64, part, 0.0)
                if s == 0:
                    part = jnp.where((wide >= at + 64) & (wide < at + 128), 0.0, part)
                v[b, 64 * s : 64 * s + 64, :] = part
            if s == 0:
                below = [w[b, pl.ds(at + 64, 64), pl.ds(o, 128)] for b in range(2)]
                below = jnp.concatenate([below[0], pltpu.roll(below[1], 64, 1)], axis=0)
                below = jnp.where(same, below, 0.0)
                lower = dot(stack6(below, 1, True), stack6(jnp.concatenate([y, y], axis=0), 1, False), 1, 1)
                lower = jnp.where(same, lower, 0.0)
                rest = [w[b, pl.ds(at + 64, 64), :] for b in range(2)]
                rest = jnp.where(here, 0.0, jnp.concatenate(rest, axis=0))
                rest = rest - dot(stack6(lower, 1, True), stack6(new, 0, False), 1, 0)
                for b in range(2):
                    w[b, pl.ds(at + 64, 64), :] = rest[64 * b : 64 * b + 64]
        here = (wide2 >= o) & (wide2 < o + 128)

        if t < 3:
            for b in range(2):
                s6[b] = stack6(v[b], 0, False)

        for i in range(t + 1, 4):
            rows = pl.ds(i * 128, 128)
            for b in range(2):
                lower = v[b, :, rows].T
                rest = jnp.where(here, 0.0, w[b, rows, :])
                w[b, rows, :] = rest - dot(stack6(lower, 1, True), s6[b], 1, 0)


def solve(x, ys, b):
    half = x.shape[1] // 2
    out = []
    for lo, depth in ((0, half), (half, 2 * half)):
        acc = None
        for y in ys:
            term = dot(x[:, :depth], y[b, lo : lo + half, :depth], 1, 1)
            acc = term if acc is None else acc + term
        out.append(acc)
    return jnp.concatenate(out, axis=1)


def panel_kernel(panel, diag, trail, cols_out, rows_out, own_out, trail_out, cols, rows, w, v, s6, hi, mid, lo, full, in_sems, *sems):
    fetch = pltpu.make_async_copy(diag, w, in_sems.at[0])
    fetch.start()
    gather = Gather(panel, cols, rows, *sems)
    gather.barrier()
    gather.start()
    fetch_trail = pltpu.make_async_copy(trail, trail_out, in_sems.at[1])
    fetch_trail.start()
    fetch.wait()

    def point(t, s, p):
        gather.point((2 * t + s) * 8 + p)

    factor(w, v, s6, point)
    ys = (hi, mid, lo)
    for b in range(2):
        hi[b], mid[b], lo[b] = split3(w[b])

    def solve_cols(group):
        slots = [gather.slot(dx, dz) for dx, dz in group]
        for b in range(2):
            x = jnp.concatenate([cols[b, i] for i in slots], axis=0)
            x = solve(x, ys[:2], b).astype(BF)
            for n, i in enumerate(slots):
                cols_out[b, i] = x[48 * n : 48 * n + 48]

    def solve_rows():
        gather.wait_rows()
        for b in range(2):
            full[b] = solve(jnp.concatenate([rows[b, i] for i in range(NC)], axis=0), ys, b)
            for i in range(NC):
                rows_out[b, i] = full[b, 48 * i : 48 * i + 48].astype(BF)
            own_out[b] = full[b, pl.ds(pl.multiple_of(gather.col * 48, 16), 48)]

    done = [e for h in sorted(PLAN) if h < LAST for e in PLAN[h]]
    late = list(PLAN[LAST])
    ready = [e[1:] for e in done if ("A",) + e[1:] in done and e[0] == "B"]
    solve_rows()
    while late or ready:
        while late and (len(ready) < 8 or len(late) > 3 * len(ready)):
            event = late.pop(0)
            gather.arrival(*event)
            done.append(event)
            if ("A",) + event[1:] in done and ("B",) + event[1:] in done:
                ready.append(event[1:])
        solve_cols(ready[:8])
        ready = ready[8:]
    gather.drain()
    fetch_trail.wait()


def panel_step(panel, diagonal, trailing):
    nb, count, k = panel.shape
    vmem = pl.BlockSpec(memory_space=pltpu.VMEM)
    hbm = pl.BlockSpec(memory_space=pltpu.HBM)
    return pl.pallas_call(
        panel_kernel,
        in_specs=[hbm] * 3,
        out_specs=[vmem] * 4,
        out_shape=[
            jax.ShapeDtypeStruct((nb, NX * NZ, count, k), BF),
            jax.ShapeDtypeStruct((nb, NC, count, k), BF),
            jax.ShapeDtypeStruct(panel.shape, F32),
            jax.ShapeDtypeStruct(trailing.shape, F32),
        ],
        scratch_shapes=[
            pltpu.VMEM((nb, NX * NZ, count, k), BF),
            pltpu.VMEM((nb, NC, count, k), BF),
            pltpu.VMEM(diagonal.shape, F32),
            pltpu.VMEM((nb, 128, k), F32),
            pltpu.VMEM((nb, 768, k), BF),
            pltpu.VMEM(diagonal.shape, BF),
            pltpu.VMEM(diagonal.shape, BF),
            pltpu.VMEM(diagonal.shape, BF),
            pltpu.VMEM((nb, NC * count, k), F32),
            DMA((2,)),
        ] + GATHER_SEMS,
        compiler_params=pltpu.CompilerParams(
            collective_id=0, has_side_effects=True, vmem_limit_bytes=42 << 20
        ),
        cost_estimate=pl.CostEstimate(flops=10**10, bytes_accessed=10**7, transcendentals=0),
        name="panel_step",
    )(*(pltpu.with_memory_space_constraint(a, pltpu.HBM) for a in (panel, diagonal, trailing)))


WIDE = 512


def update_kernel(pat, cols, rows, own, trail, out, solved, buf, own_buf, sems, own_sem):
    row, col = lax.axis_index("row"), lax.axis_index("col")
    nb, m, n = buf.shape
    count = own.shape[1]
    first = (row * NC + col) * count
    low, high = first // BLK, (first + count - 1) // BLK
    at = first + lax.broadcasted_iota(jnp.int32, own.shape[1:], 0)
    keep = jnp.where(at < high * BLK, pat[low], pat[high]).astype(F32)
    for b in range(nb):
        own_buf[b] = own[b] * keep
    own_copy = pltpu.make_async_copy(own_buf, solved, own_sem)
    own_copy.start()
    keep_rows = [pat[row * (m // BLK) + i] for i in range(m // BLK)]
    copies = []
    for b in range(nb):
        for j in range(n // WIDE):
            there = pl.ds(j * WIDE, WIDE)
            prod = dot(rows[b], cols[b, there], 1, 1)
            for q in range(WIDE // BLK):
                keep_col = pat[col * (n // BLK) + j * (WIDE // BLK) + q]
                for i, keep_row in enumerate(keep_rows):
                    r = slice(i * BLK, (i + 1) * BLK)
                    c = slice(j * WIDE + q * BLK, j * WIDE + (q + 1) * BLK)
                    both = (keep_col * keep_row).astype(F32)
                    buf[b, r, c] = trail[b, r, c] - both * prod[r, q * BLK : (q + 1) * BLK]
            copy = pltpu.make_async_copy(buf.at[b, :, there], out.at[b, :, there], sems.at[b, j])
            copy.start()
            copies.append(copy)
    for copy in copies:
        copy.wait()
    own_copy.wait()


def update(pattern, cols, rows, own, trailing):
    vmem = pl.BlockSpec(memory_space=pltpu.VMEM)
    hbm = pl.BlockSpec(memory_space=pltpu.HBM)
    nb, m, n = trailing.shape
    return pl.pallas_call(
        update_kernel,
        in_specs=[pl.BlockSpec(memory_space=pltpu.SMEM)] + [vmem] * 4,
        out_specs=[hbm] * 2,
        out_shape=[jax.ShapeDtypeStruct(trailing.shape, F32), jax.ShapeDtypeStruct(own.shape, F32)],
        scratch_shapes=[
            pltpu.VMEM(trailing.shape, F32),
            pltpu.VMEM(own.shape, F32),
            DMA((nb, n // WIDE)),
            DMA,
        ],
        compiler_params=pltpu.CompilerParams(vmem_limit_bytes=36 << 20),
        cost_estimate=pl.CostEstimate(flops=10**9, bytes_accessed=10**7, transcendentals=0),
        name="update",
    )(pattern, cols, rows, own, trailing)


def per_device(trailing, panel, diagonal, pattern):
    cols, rows, own, trail = panel_step(panel, diagonal, trailing)
    nb, _, _, k = cols.shape
    return tuple(update(pattern, cols.reshape(nb, -1, k), rows.reshape(nb, -1, k), own, trail))


def solution(mesh):
    return jax.shard_map(
        per_device,
        mesh=mesh,
        in_specs=(P(None, "row", "col"), P(None, ("row", "col"), None), P(), P()),
        out_specs=(P(None, "row", "col"), P(None, ("row", "col"), None)),
        check_vma=False,
    )
```

```python
import functools

import jax
import jax.numpy as jnp
from jax import lax
from jax.experimental import pallas as pl
from jax.experimental.pallas import tpu as pltpu
from jax.sharding import PartitionSpec as P

BLK = 128
F32 = jnp.float32
BF = jnp.bfloat16
HIGHEST = lax.Precision.HIGHEST
MESH = pl.DeviceIdType.MESH
NX, NZ, NC = 4, 8, 8

PLAN = {
    3: [('A', 0, 0)],
    5: [('B', 0, 0)],
    10: [('A', 1, 0), ('A', -1, 0), ('A', 0, 1), ('A', 0, -1)],
    14: [('B', 1, 0), ('B', -1, 0), ('B', 0, 1), ('B', 0, -1)],
    17: [('A', 2, 0)],
    22: [('A', 1, 1), ('A', -1, 1), ('A', 0, 2), ('A', 1, -1), ('A', -1, -1), ('A', 0, -2)],
    26: [('A', 2, 1), ('A', 2, -1)],
    27: [('B', 0, 2), ('B', 0, -2), ('B', -1, 1), ('B', -1, -1)],
    31: [('B', 2, 0), ('B', 1, 1), ('B', 1, -1)],
    34: [('A', 1, 2), ('A', -1, 2), ('A', 0, 3), ('A', 1, -2), ('A', -1, -2), ('A', 0, -3)],
    37: [('A', 2, 2), ('A', 2, -2)],
    39: [('B', 0, 3), ('B', 0, -3)],
    40: [('B', 1, 2), ('B', 1, -2)],
    44: [('A', 1, -3), ('A', -1, -3)],
    45: [('A', 2, -3)],
    46: [('A', 1, 3), ('A', -1, 3), ('A', 0, 4)],
    48: [('A', 2, 3)],
    49: [('B', -1, 2), ('B', -1, -2), ('B', 2, 1), ('B', 2, -1)],
    51: [('B', 0, 4)],
    52: [('A', -1, 4)],
    53: [('A', 2, 4), ('A', 1, 4)],
    55: [('B', -1, 3), ('B', -1, -3)],
    59: [('B', 1, 3), ('B', 1, -3)],
    60: [('B', 2, 2), ('B', 2, -2), ('B', -1, 4)],
    63: [('B', 1, 4)],
    64: [('B', 2, 3), ('B', 2, -3), ('B', 2, 4)],
}
LAST = 64
ROWS_AT = 8
PART = {"A": (0, 16), "B": (16, 32)}


def onward(part, dx, dz):
    out = []
    along_x = part == "B" or dz == 0
    along_z = part == "A" or dx == 0
    if along_x:
        if dx == 0:
            out += [("x", 1, 1, dz), ("x", -1, -1, dz)]
        elif dx == 1 and (part == "A" or dz % 2 == 0):
            out += [("x", 1, 2, dz)]
        elif dx == -1 and part == "B" and dz % 2 == 1:
            out += [("x", -1, 2, dz)]
    if along_z:
        if dz == 0:
            out += [("z", 1, dx, 1), ("z", -1, dx, -1)]
        elif 0 < dz < 3 or (dz == 3 and (part == "B" or dx in (0, 1))):
            out += [("z", 1, dx, dz + 1)]
        elif -3 < dz < 0 or (dz == -3 and part == "A" and dx in (2, -1)):
            out += [("z", -1, dx, dz - 1 if dz > -3 else 4)]
    return out


def rel(dx, dz):
    return (dx % NX) * NZ + dz % NZ


class Gather:
    def __init__(self, panel, cols, rows, first_sem, arrive_sem, send_sem, recv_sem, row_send, row_recv, own_sem):
        self.panel, self.cols, self.rows = panel, cols, rows
        self.first_sem, self.arrive_sem = first_sem, arrive_sem
        self.send_sem, self.recv_sem = send_sem, recv_sem
        self.row_send, self.row_recv, self.own_sem = row_send, row_recv, own_sem
        self.row, self.col = lax.axis_index("row"), lax.axis_index("col")
        self.x, self.z = self.row // NZ, self.row % NZ
        self.y, self.k = self.col // 2, self.col % 2
        x, y, z, k = self.x, self.y, self.z, self.k
        self.to_row = ((x + y) % NX) * NZ + (2 * (z % 4) + k + 6 + 4 * (z // 4)) % NZ
        self.to_col = 2 * x + z // 4
        self.to_slot = (z % 4) * NC + self.col
        u = (z + 10 - 4 * k) % NZ
        self.from_row = y * NZ + 4 * k + u // 2
        self.from_col = ((x + NX - y) % NX) * 2 + u % 2
        self.stays = (self.to_row == self.row) & (self.to_col == self.col)
        self.moves = jnp.logical_not(self.stays)
        self.slot_x = [((x + 2 * NX - dx - y) % NX) * 2 for dx in range(NX)]
        us = [(z + 10 + NZ - dz - 4 * k) % NZ for dz in range(NZ)]
        self.slot_z = [(u // 2) * NC + u % 2 for u in us]
        self.home = self.slot(0, 0)
        self.near = {}
        for step in (1, -1):
            self.near["x", step] = (((x + step + NX) % NX) * NZ + z, self.col)
            self.near["z", step] = (x * NZ + (z + step + NZ) % NZ, self.col)
        self.sent = []

    def slot(self, dx, dz):
        return self.slot_x[dx % NX] + self.slot_z[dz % NZ]

    def neighbour(self, axis, step):
        return self.near[axis, step]

    def peer(self, i):
        return (self.row, (self.col + i) % NC)

    def barrier(self):
        sem = pltpu.get_barrier_semaphore()
        near = list(self.near.values()) + [self.peer(i) for i in range(1, NC)]
        for d in near:
            pl.semaphore_signal(sem, inc=1, device_id=d, device_id_type=MESH)

        @pl.when(self.moves)
        def _():
            for d in ((self.to_row, self.to_col), (self.from_row, self.from_col)):
                pl.semaphore_signal(sem, inc=1, device_id=d, device_id_type=MESH)
            pl.semaphore_wait(sem, len(near) + 2)

        pl.when(self.stays)(lambda: pl.semaphore_wait(sem, len(near)))

    def first(self, part, slot):
        i = 0 if part == "A" else 1
        return pltpu.make_async_remote_copy(
            self.panel.at[:, pl.ds(*PART[part])], self.piece(part, slot),
            self.first_sem.at[i], self.arrive_sem.at[i],
            device_id=(self.to_row, self.to_col), device_id_type=MESH,
        )

    def first_stays(self, part):
        return pltpu.make_async_copy(
            self.panel.at[:, pl.ds(*PART[part])], self.piece(part, self.home),
            self.first_sem.at[0 if part == "A" else 1],
        )

    def row_copy(self, i, col):
        return pltpu.make_async_remote_copy(
            self.panel, self.rows.at[:, col], self.row_send.at[i], self.row_recv.at[i],
            device_id=self.peer(i + 1), device_id_type=MESH,
        )

    def row_own(self):
        return pltpu.make_async_copy(self.panel, self.rows.at[:, self.col], self.own_sem)

    def start(self):
        for part in PART:
            pl.when(self.moves)(lambda: self.first(part, self.to_slot).start())
            pl.when(self.stays)(lambda: self.first_stays(part).start())

    def start_rows(self):
        for i in range(NC - 1):
            self.row_copy(i, self.col).start()
        self.row_own().start()

    def piece(self, part, slot):
        return self.cols.at[:, slot, pl.ds(*PART[part])]

    def move(self, part, slot, i, dx, dz, to):
        ref = self.piece(part, slot)
        return pltpu.make_async_remote_copy(
            ref, ref, self.send_sem.at[i], self.recv_sem.at[0 if part == "A" else 1, rel(dx, dz)],
            device_id=to, device_id_type=MESH,
        )

    def arrival(self, part, dx, dz):
        slot = self.slot(dx, dz)
        if (dx, dz) != (0, 0):
            self.move(part, slot, 0, dx, dz, self.neighbour("x", 1)).wait_recv()
        else:
            pl.when(self.moves)(lambda: self.first(part, self.home).wait_recv())
            pl.when(self.stays)(lambda: self.first_stays(part).wait())
        for axis, step, ndx, ndz in onward(part, dx, dz):
            self.move(part, slot, len(self.sent), ndx, ndz, self.neighbour(axis, step)).start()
            self.sent.append(part)

    def point(self, h):
        if h == ROWS_AT:
            self.start_rows()
        for part, dx, dz in PLAN.get(h, ()):
            self.arrival(part, dx, dz)

    def wait_rows(self):
        for i in range(NC - 1):
            self.row_copy(i, (self.col + NC - 1 - i) % NC).wait_recv()
        self.row_own().wait()

    def drain(self):
        for i, part in enumerate(self.sent):
            self.move(part, self.home, i, 0, 0, self.neighbour("x", 1)).wait_send()
        for part in PART:
            pl.when(self.moves)(lambda: self.first(part, self.to_slot).wait_send())
        for i in range(NC - 1):
            self.row_copy(i, self.col).wait_send()


DMA = pltpu.SemaphoreType.DMA
GATHER_SEMS = [DMA((2,)), DMA((2,)), DMA((62,)), DMA((2, NX * NZ)), DMA((NC - 1,)), DMA((NC - 1,)), DMA]


def dot(a, b, ca, cb, precision=None):
    return lax.dot_general(
        a, b, (((ca,), (cb,)), ((), ())), precision=precision, preferred_element_type=F32
    )


def split3(x):
    hi = x.astype(BF)
    rest = x - hi.astype(F32)
    mid = rest.astype(BF)
    return hi, mid, (rest - mid.astype(F32)).astype(BF)


def stack6(x, axis, left):
    h, m, l = split3(x)
    return jnp.concatenate([h, h, m, h, l, m] if left else [h, m, h, l, h, m], axis=axis)


def spread(x, k):
    return jnp.broadcast_to(x[k : k + 1, :], (8, 128))


def base(x, point):
    lane = lax.broadcasted_iota(jnp.int32, (8, 128), 1)
    sub = lax.broadcasted_iota(jnp.int32, (8, 128), 0)
    half = jnp.where(lane < 64, 0, 64)
    x = list(x)
    e = [jnp.where(lane - half == sub + 8 * g, 1.0, 0.0).astype(F32) for g in range(8)]
    out = []
    for p in range(8):
        point(p)
        t = {
            g: [
                jnp.take_along_axis(x[g], half + (8 * p + c), axis=1, mode="promise_in_bounds")
                for c in range(8)
            ]
            for g in range(p, 8)
        }
        pivots = t[p][0]
        for k in range(8):
            d = spread(t[p][k], k)
            pivots = jnp.where(sub == k, d, pivots)
            r = 1.0 / d
            pe, px = spread(e[p], k), spread(x[p], k)
            top = {c: spread(t[p][c], k) for c in range(k + 1, 8)}
            for g in range(p, 8):
                if g == p and k == 7:
                    continue
                m = t[g][k] * r
                if g == p:
                    m = jnp.where(sub > k, m, 0.0)
                for c in range(k + 1, 8):
                    if g == p and c == k + 1:
                        t[g][c] = t[g][c] - jnp.where(sub > k, t[g][k] * top[c], 0.0) * r
                    else:
                        t[g][c] = t[g][c] - m * top[c]
                if p < 7:
                    x[g] = x[g] - m * px
                e[g] = e[g] - m * pe
        out.append(e[p] * lax.rsqrt(pivots))
    return jnp.concatenate(out, axis=0)


def factor(w, v, s6, point):
    lane = lax.broadcasted_iota(jnp.int32, (8, 128), 1)
    wide = lax.broadcasted_iota(jnp.int32, (64, 512), 1)
    wide2 = lax.broadcasted_iota(jnp.int32, (128, 512), 1)
    band = lax.broadcasted_iota(jnp.int32, (128, 128), 0) // 64
    same = band == lax.broadcasted_iota(jnp.int32, (128, 128), 1) // 64

    for t in range(4):
        o = t * 128
        for s in range(2):
            at = o + 64 * s
            x = []
            for g in range(8):
                rows = pl.ds(at + 8 * g, 8)
                a, b = w[0, rows, pl.ds(o, 128)], w[1, rows, pl.ds(o, 128)]
                if s == 0:
                    x.append(jnp.where(lane < 64, a, pltpu.roll(b, 64, 1)))
                else:
                    x.append(jnp.where(lane < 64, pltpu.roll(a, 64, 1), b))
            y = base(x, functools.partial(point, t, s))
            both = jnp.concatenate([w[0, pl.ds(at, 64), :], w[1, pl.ds(at, 64), :]], axis=0)
            ys = jnp.where(same, jnp.concatenate([y, y], axis=0), 0.0)
            new = dot(stack6(ys, 1, True), stack6(both, 0, False), 1, 0)
            here = (wide2 >= at) & (wide2 < at + 64)
            yt = jnp.where(same, ys, pltpu.roll(ys, 64, 1))
            yt = jnp.concatenate([yt] * 4, axis=1)
            new = jnp.where(here, yt, new)
            for b in range(2):
                part = new[64 * b : 64 * b + 64]
                w[b, pl.ds(at, 64), :] = jnp.where(wide < at + 64, part, 0.0)
                if s == 0:
                    part = jnp.where((wide >= at + 64) & (wide < at + 128), 0.0, part)
                v[b, 64 * s : 64 * s + 64, :] = part
            if s == 0:
                below = [w[b, pl.ds(at + 64, 64), pl.ds(o, 128)] for b in range(2)]
                below = jnp.concatenate([below[0], pltpu.roll(below[1], 64, 1)], axis=0)
                below = jnp.where(same, below, 0.0)
                lower = dot(stack6(below, 1, True), stack6(jnp.concatenate([y, y], axis=0), 1, False), 1, 1)
                lower = jnp.where(same, lower, 0.0)
                rest = [w[b, pl.ds(at + 64, 64), :] for b in range(2)]
                rest = jnp.where(here, 0.0, jnp.concatenate(rest, axis=0))
                rest = rest - dot(stack6(lower, 1, True), stack6(new, 0, False), 1, 0)
                for b in range(2):
                    w[b, pl.ds(at + 64, 64), :] = rest[64 * b : 64 * b + 64]
        here = (wide2 >= o) & (wide2 < o + 128)

        if t < 3:
            for b in range(2):
                s6[b] = stack6(v[b], 0, False)

        for i in range(t + 1, 4):
            rows = pl.ds(i * 128, 128)
            for b in range(2):
                lower = v[b, :, rows].T
                rest = jnp.where(here, 0.0, w[b, rows, :])
                w[b, rows, :] = rest - dot(stack6(lower, 1, True), s6[b], 1, 0)


def solve(x, ys, b):
    half = x.shape[1] // 2
    out = []
    for lo, depth in ((0, half), (half, 2 * half)):
        acc = None
        for y in ys:
            term = dot(x[:, :depth], y[b, lo : lo + half, :depth], 1, 1)
            acc = term if acc is None else acc + term
        out.append(acc)
    return jnp.concatenate(out, axis=1)


def panel_kernel(panel, diag, trail, cols_out, rows_out, own_out, trail_out, cols, rows, w, v, s6, hi, mid, lo, full, in_sems, *sems):
    fetch = pltpu.make_async_copy(diag, w, in_sems.at[0])
    fetch.start()
    gather = Gather(panel, cols, rows, *sems)
    gather.barrier()
    gather.start()
    fetch_trail = pltpu.make_async_copy(trail, trail_out, in_sems.at[1])
    fetch_trail.start()
    fetch.wait()

    def point(t, s, p):
        gather.point((2 * t + s) * 8 + p)

    factor(w, v, s6, point)
    ys = (hi, mid, lo)
    for b in range(2):
        hi[b], mid[b], lo[b] = split3(w[b])

    def solve_cols(group):
        slots = [gather.slot(dx, dz) for dx, dz in group]
        for b in range(2):
            x = jnp.concatenate([cols[b, i] for i in slots], axis=0)
            x = solve(x, ys[:2], b).astype(BF)
            for n, i in enumerate(slots):
                cols_out[b, i] = x[48 * n : 48 * n + 48]

    def solve_rows():
        gather.wait_rows()
        for b in range(2):
            full[b] = solve(jnp.concatenate([rows[b, i] for i in range(NC)], axis=0), ys, b)
            for i in range(NC):
                rows_out[b, i] = full[b, 48 * i : 48 * i + 48].astype(BF)
            own_out[b] = full[b, pl.ds(pl.multiple_of(gather.col * 48, 16), 48)]

    done = [e for h in sorted(PLAN) if h < LAST for e in PLAN[h]]
    late = list(PLAN.get(LAST, ()))
    ready = [e[1:] for e in done if ("A",) + e[1:] in done and e[0] == "B"]
    solve_rows()
    while late or ready:
        while late and (len(ready) < 8 or len(late) > 3 * len(ready)):
            event = late.pop(0)
            gather.arrival(*event)
            done.append(event)
            if ("A",) + event[1:] in done and ("B",) + event[1:] in done:
                ready.append(event[1:])
        solve_cols(ready[:8])
        ready = ready[8:]
    gather.drain()
    fetch_trail.wait()


def panel_step(panel, diagonal, trailing):
    nb, count, k = panel.shape
    vmem = pl.BlockSpec(memory_space=pltpu.VMEM)
    hbm = pl.BlockSpec(memory_space=pltpu.HBM)
    return pl.pallas_call(
        panel_kernel,
        in_specs=[hbm] * 3,
        out_specs=[vmem] * 4,
        out_shape=[
            jax.ShapeDtypeStruct((nb, NX * NZ, count, k), BF),
            jax.ShapeDtypeStruct((nb, NC, count, k), BF),
            jax.ShapeDtypeStruct(panel.shape, F32),
            jax.ShapeDtypeStruct(trailing.shape, F32),
        ],
        scratch_shapes=[
            pltpu.VMEM((nb, NX * NZ, count, k), BF),
            pltpu.VMEM((nb, NC, count, k), BF),
            pltpu.VMEM(diagonal.shape, F32),
            pltpu.VMEM((nb, 128, k), F32),
            pltpu.VMEM((nb, 768, k), BF),
            pltpu.VMEM(diagonal.shape, BF),
            pltpu.VMEM(diagonal.shape, BF),
            pltpu.VMEM(diagonal.shape, BF),
            pltpu.VMEM((nb, NC * count, k), F32),
            DMA((2,)),
        ] + GATHER_SEMS,
        compiler_params=pltpu.CompilerParams(
            collective_id=0, has_side_effects=True, vmem_limit_bytes=42 << 20
        ),
        cost_estimate=pl.CostEstimate(flops=10**10, bytes_accessed=10**7, transcendentals=0),
        name="panel_step",
    )(*(pltpu.with_memory_space_constraint(a, pltpu.HBM) for a in (panel, diagonal, trailing)))


WIDE = 512


def update_kernel(pat, cols, rows, own, trail, out, solved, buf, own_buf, sems, own_sem):
    row, col = lax.axis_index("row"), lax.axis_index("col")
    nb, m, n = buf.shape
    count = own.shape[1]
    first = (row * NC + col) * count
    low, high = first // BLK, (first + count - 1) // BLK
    at = first + lax.broadcasted_iota(jnp.int32, own.shape[1:], 0)
    keep = jnp.where(at < high * BLK, pat[low], pat[high]).astype(F32)
    for b in range(nb):
        own_buf[b] = own[b] * keep
    own_copy = pltpu.make_async_copy(own_buf, solved, own_sem)
    own_copy.start()
    keep_rows = [pat[row * (m // BLK) + i] for i in range(m // BLK)]
    copies = []
    for b in range(nb):
        for j in range(n // WIDE):
            there = pl.ds(j * WIDE, WIDE)
            prod = dot(rows[b], cols[b, there], 1, 1)
            for q in range(WIDE // BLK):
                keep_col = pat[col * (n // BLK) + j * (WIDE // BLK) + q]
                for i, keep_row in enumerate(keep_rows):
                    r = slice(i * BLK, (i + 1) * BLK)
                    c = slice(j * WIDE + q * BLK, j * WIDE + (q + 1) * BLK)
                    both = (keep_col * keep_row).astype(F32)
                    buf[b, r, c] = trail[b, r, c] - both * prod[r, q * BLK : (q + 1) * BLK]
            copy = pltpu.make_async_copy(buf.at[b, :, there], out.at[b, :, there], sems.at[b, j])
            copy.start()
            copies.append(copy)
    for copy in copies:
        copy.wait()
    own_copy.wait()


def update(pattern, cols, rows, own, trailing):
    vmem = pl.BlockSpec(memory_space=pltpu.VMEM)
    hbm = pl.BlockSpec(memory_space=pltpu.HBM)
    nb, m, n = trailing.shape
    return pl.pallas_call(
        update_kernel,
        in_specs=[pl.BlockSpec(memory_space=pltpu.SMEM)] + [vmem] * 4,
        out_specs=[hbm] * 2,
        out_shape=[jax.ShapeDtypeStruct(trailing.shape, F32), jax.ShapeDtypeStruct(own.shape, F32)],
        scratch_shapes=[
            pltpu.VMEM(trailing.shape, F32),
            pltpu.VMEM(own.shape, F32),
            DMA((nb, n // WIDE)),
            DMA,
        ],
        compiler_params=pltpu.CompilerParams(vmem_limit_bytes=36 << 20),
        cost_estimate=pl.CostEstimate(flops=10**9, bytes_accessed=10**7, transcendentals=0),
        name="update",
    )(pattern, cols, rows, own, trailing)


def per_device(trailing, panel, diagonal, pattern):
    cols, rows, own, trail = panel_step(panel, diagonal, trailing)
    nb, _, _, k = cols.shape
    return tuple(update(pattern, cols.reshape(nb, -1, k), rows.reshape(nb, -1, k), own, trail))


def solution(mesh):
    return jax.shard_map(
        per_device,
        mesh=mesh,
        in_specs=(P(None, "row", "col"), P(None, ("row", "col"), None), P(), P()),
        out_specs=(P(None, "row", "col"), P(None, ("row", "col"), None)),
        check_vma=False,
    )
```

```python
import functools

import jax
import jax.numpy as jnp
from jax import lax
from jax.experimental import pallas as pl
from jax.experimental.pallas import tpu as pltpu
from jax.sharding import PartitionSpec as P

BLK = 128
F32 = jnp.float32
BF = jnp.bfloat16
HIGHEST = lax.Precision.HIGHEST
MESH = pl.DeviceIdType.MESH
NX, NZ, NC = 4, 8, 8

PLAN = {
    3: [('A', 0, 0)],
    5: [('B', 0, 0)],
    10: [('A', 1, 0), ('A', -1, 0), ('A', 0, 1), ('A', 0, -1)],
    14: [('B', 1, 0), ('B', -1, 0), ('B', 0, 1), ('B', 0, -1)],
    17: [('A', 2, 0)],
    22: [('A', 1, 1), ('A', -1, 1), ('A', 0, 2), ('A', 1, -1), ('A', -1, -1), ('A', 0, -2)],
    26: [('A', 2, 1), ('A', 2, -1)],
    27: [('B', 0, 2), ('B', 0, -2), ('B', -1, 1), ('B', -1, -1)],
    31: [('B', 2, 0), ('B', 1, 1), ('B', 1, -1)],
    34: [('A', 1, 2), ('A', -1, 2), ('A', 0, 3), ('A', 1, -2), ('A', -1, -2), ('A', 0, -3)],
    37: [('A', 2, 2), ('A', 2, -2)],
    39: [('B', 0, 3), ('B', 0, -3)],
    40: [('B', 1, 2), ('B', 1, -2)],
    44: [('A', 1, -3), ('A', -1, -3)],
    45: [('A', 2, -3)],
    46: [('A', 1, 3), ('A', -1, 3), ('A', 0, 4)],
    48: [('A', 2, 3)],
    49: [('B', -1, 2), ('B', -1, -2), ('B', 2, 1), ('B', 2, -1)],
    51: [('B', 0, 4)],
    52: [('A', -1, 4)],
    53: [('A', 2, 4), ('A', 1, 4)],
    55: [('B', -1, 3), ('B', -1, -3)],
    59: [('B', 1, 3), ('B', 1, -3)],
    60: [('B', 2, 2), ('B', 2, -2), ('B', -1, 4)],
    63: [('B', 1, 4)],
    64: [('B', 2, 3), ('B', 2, -3), ('B', 2, 4)],
}
LAST = 64
ROWS_AT = 16
PART = {"A": (0, 16), "B": (16, 32)}


def onward(part, dx, dz):
    out = []
    along_x = part == "B" or dz == 0
    along_z = part == "A" or dx == 0
    if along_x:
        if dx == 0:
            out += [("x", 1, 1, dz), ("x", -1, -1, dz)]
        elif dx == 1 and (part == "A" or dz % 2 == 0):
            out += [("x", 1, 2, dz)]
        elif dx == -1 and part == "B" and dz % 2 == 1:
            out += [("x", -1, 2, dz)]
    if along_z:
        if dz == 0:
            out += [("z", 1, dx, 1), ("z", -1, dx, -1)]
        elif 0 < dz < 3 or (dz == 3 and (part == "B" or dx in (0, 1))):
            out += [("z", 1, dx, dz + 1)]
        elif -3 < dz < 0 or (dz == -3 and part == "A" and dx in (2, -1)):
            out += [("z", -1, dx, dz - 1 if dz > -3 else 4)]
    return out


def rel(dx, dz):
    return (dx % NX) * NZ + dz % NZ


class Gather:
    def __init__(self, panel, cols, rows, first_sem, arrive_sem, send_sem, recv_sem, row_send, row_recv, own_sem):
        self.panel, self.cols, self.rows = panel, cols, rows
        self.first_sem, self.arrive_sem = first_sem, arrive_sem
        self.send_sem, self.recv_sem = send_sem, recv_sem
        self.row_send, self.row_recv, self.own_sem = row_send, row_recv, own_sem
        self.row, self.col = lax.axis_index("row"), lax.axis_index("col")
        self.x, self.z = self.row // NZ, self.row % NZ
        self.y, self.k = self.col // 2, self.col % 2
        x, y, z, k = self.x, self.y, self.z, self.k
        self.to_row = ((x + y) % NX) * NZ + (2 * (z % 4) + k + 6 + 4 * (z // 4)) % NZ
        self.to_col = 2 * x + z // 4
        self.to_slot = (z % 4) * NC + self.col
        u = (z + 10 - 4 * k) % NZ
        self.from_row = y * NZ + 4 * k + u // 2
        self.from_col = ((x + NX - y) % NX) * 2 + u % 2
        self.stays = (self.to_row == self.row) & (self.to_col == self.col)
        self.moves = jnp.logical_not(self.stays)
        self.slot_x = [((x + 2 * NX - dx - y) % NX) * 2 for dx in range(NX)]
        us = [(z + 10 + NZ - dz - 4 * k) % NZ for dz in range(NZ)]
        self.slot_z = [(u // 2) * NC + u % 2 for u in us]
        self.home = self.slot(0, 0)
        self.near = {}
        for step in (1, -1):
            self.near["x", step] = (((x + step + NX) % NX) * NZ + z, self.col)
            self.near["z", step] = (x * NZ + (z + step + NZ) % NZ, self.col)
        self.sent = []

    def slot(self, dx, dz):
        return self.slot_x[dx % NX] + self.slot_z[dz % NZ]

    def neighbour(self, axis, step):
        return self.near[axis, step]

    def peer(self, i):
        return (self.row, (self.col + i) % NC)

    def barrier(self):
        sem = pltpu.get_barrier_semaphore()
        near = list(self.near.values()) + [self.peer(i) for i in range(1, NC)]
        for d in near:
            pl.semaphore_signal(sem, inc=1, device_id=d, device_id_type=MESH)

        @pl.when(self.moves)
        def _():
            for d in ((self.to_row, self.to_col), (self.from_row, self.from_col)):
                pl.semaphore_signal(sem, inc=1, device_id=d, device_id_type=MESH)
            pl.semaphore_wait(sem, len(near) + 2)

        pl.when(self.stays)(lambda: pl.semaphore_wait(sem, len(near)))

    def first(self, part, slot):
        i = 0 if part == "A" else 1
        return pltpu.make_async_remote_copy(
            self.panel.at[:, pl.ds(*PART[part])], self.piece(part, slot),
            self.first_sem.at[i], self.arrive_sem.at[i],
            device_id=(self.to_row, self.to_col), device_id_type=MESH,
        )

    def first_stays(self, part):
        return pltpu.make_async_copy(
            self.panel.at[:, pl.ds(*PART[part])], self.piece(part, self.home),
            self.first_sem.at[0 if part == "A" else 1],
        )

    def row_copy(self, i, col):
        return pltpu.make_async_remote_copy(
            self.panel, self.rows.at[:, col], self.row_send.at[i], self.row_recv.at[i],
            device_id=self.peer(i + 1), device_id_type=MESH,
        )

    def row_own(self):
        return pltpu.make_async_copy(self.panel, self.rows.at[:, self.col], self.own_sem)

    def start(self):
        for part in PART:
            pl.when(self.moves)(lambda: self.first(part, self.to_slot).start())
            pl.when(self.stays)(lambda: self.first_stays(part).start())

    def start_rows(self):
        for i in range(NC - 1):
            self.row_copy(i, self.col).start()
        self.row_own().start()

    def piece(self, part, slot):
        return self.cols.at[:, slot, pl.ds(*PART[part])]

    def move(self, part, slot, i, dx, dz, to):
        ref = self.piece(part, slot)
        return pltpu.make_async_remote_copy(
            ref, ref, self.send_sem.at[i], self.recv_sem.at[0 if part == "A" else 1, rel(dx, dz)],
            device_id=to, device_id_type=MESH,
        )

    def arrival(self, part, dx, dz):
        slot = self.slot(dx, dz)
        if (dx, dz) != (0, 0):
            self.move(part, slot, 0, dx, dz, self.neighbour("x", 1)).wait_recv()
        else:
            pl.when(self.moves)(lambda: self.first(part, self.home).wait_recv())
            pl.when(self.stays)(lambda: self.first_stays(part).wait())
        for axis, step, ndx, ndz in onward(part, dx, dz):
            self.move(part, slot, len(self.sent), ndx, ndz, self.neighbour(axis, step)).start()
            self.sent.append(part)

    def point(self, h):
        if h == ROWS_AT:
            self.start_rows()
        for part, dx, dz in PLAN.get(h, ()):
            self.arrival(part, dx, dz)

    def wait_rows(self):
        for i in range(NC - 1):
            self.row_copy(i, (self.col + NC - 1 - i) % NC).wait_recv()
        self.row_own().wait()

    def drain(self):
        for i, part in enumerate(self.sent):
            self.move(part, self.home, i, 0, 0, self.neighbour("x", 1)).wait_send()
        for part in PART:
            pl.when(self.moves)(lambda: self.first(part, self.to_slot).wait_send())
        for i in range(NC - 1):
            self.row_copy(i, self.col).wait_send()


DMA = pltpu.SemaphoreType.DMA
GATHER_SEMS = [DMA((2,)), DMA((2,)), DMA((62,)), DMA((2, NX * NZ)), DMA((NC - 1,)), DMA((NC - 1,)), DMA]


def dot(a, b, ca, cb, precision=None):
    return lax.dot_general(
        a, b, (((ca,), (cb,)), ((), ())), precision=precision, preferred_element_type=F32
    )


def split3(x):
    hi = x.astype(BF)
    rest = x - hi.astype(F32)
    mid = rest.astype(BF)
    return hi, mid, (rest - mid.astype(F32)).astype(BF)


def stack6(x, axis, left):
    h, m, l = split3(x)
    return jnp.concatenate([h, h, m, h, l, m] if left else [h, m, h, l, h, m], axis=axis)


def spread(x, k):
    return jnp.broadcast_to(x[k : k + 1, :], (8, 128))


def base(x, point):
    lane = lax.broadcasted_iota(jnp.int32, (8, 128), 1)
    sub = lax.broadcasted_iota(jnp.int32, (8, 128), 0)
    half = jnp.where(lane < 64, 0, 64)
    x = list(x)
    e = [jnp.where(lane - half == sub + 8 * g, 1.0, 0.0).astype(F32) for g in range(8)]
    out = []
    for p in range(8):
        point(p)
        t = {
            g: [
                jnp.take_along_axis(x[g], half + (8 * p + c), axis=1, mode="promise_in_bounds")
                for c in range(8)
            ]
            for g in range(p, 8)
        }
        pivots = t[p][0]
        for k in range(8):
            d = spread(t[p][k], k)
            pivots = jnp.where(sub == k, d, pivots)
            r = 1.0 / d
            pe, px = spread(e[p], k), spread(x[p], k)
            top = {c: spread(t[p][c], k) for c in range(k + 1, 8)}
            for g in range(p, 8):
                if g == p and k == 7:
                    continue
                m = t[g][k] * r
                if g == p:
                    m = jnp.where(sub > k, m, 0.0)
                for c in range(k + 1, 8):
                    if g == p and c == k + 1:
                        t[g][c] = t[g][c] - jnp.where(sub > k, t[g][k] * top[c], 0.0) * r
                    else:
                        t[g][c] = t[g][c] - m * top[c]
                if p < 7:
                    x[g] = x[g] - m * px
                e[g] = e[g] - m * pe
        out.append(e[p] * lax.rsqrt(pivots))
    return jnp.concatenate(out, axis=0)


def factor(w, v, s6, point):
    lane = lax.broadcasted_iota(jnp.int32, (8, 128), 1)
    wide = lax.broadcasted_iota(jnp.int32, (64, 512), 1)
    wide2 = lax.broadcasted_iota(jnp.int32, (128, 512), 1)
    band = lax.broadcasted_iota(jnp.int32, (128, 128), 0) // 64
    same = band == lax.broadcasted_iota(jnp.int32, (128, 128), 1) // 64

    for t in range(4):
        o = t * 128
        for s in range(2):
            at = o + 64 * s
            x = []
            for g in range(8):
                rows = pl.ds(at + 8 * g, 8)
                a, b = w[0, rows, pl.ds(o, 128)], w[1, rows, pl.ds(o, 128)]
                if s == 0:
                    x.append(jnp.where(lane < 64, a, pltpu.roll(b, 64, 1)))
                else:
                    x.append(jnp.where(lane < 64, pltpu.roll(a, 64, 1), b))
            y = base(x, functools.partial(point, t, s))
            both = jnp.concatenate([w[0, pl.ds(at, 64), :], w[1, pl.ds(at, 64), :]], axis=0)
            ys = jnp.where(same, jnp.concatenate([y, y], axis=0), 0.0)
            new = dot(stack6(ys, 1, True), stack6(both, 0, False), 1, 0)
            here = (wide2 >= at) & (wide2 < at + 64)
            yt = jnp.where(same, ys, pltpu.roll(ys, 64, 1))
            yt = jnp.concatenate([yt] * 4, axis=1)
            new = jnp.where(here, yt, new)
            for b in range(2):
                part = new[64 * b : 64 * b + 64]
                w[b, pl.ds(at, 64), :] = jnp.where(wide < at + 64, part, 0.0)
                if s == 0:
                    part = jnp.where((wide >= at + 64) & (wide < at + 128), 0.0, part)
                v[b, 64 * s : 64 * s + 64, :] = part
            if s == 0:
                below = [w[b, pl.ds(at + 64, 64), pl.ds(o, 128)] for b in range(2)]
                below = jnp.concatenate([below[0], pltpu.roll(below[1], 64, 1)], axis=0)
                below = jnp.where(same, below, 0.0)
                lower = dot(stack6(below, 1, True), stack6(jnp.concatenate([y, y], axis=0), 1, False), 1, 1)
                lower = jnp.where(same, lower, 0.0)
                rest = [w[b, pl.ds(at + 64, 64), :] for b in range(2)]
                rest = jnp.where(here, 0.0, jnp.concatenate(rest, axis=0))
                rest = rest - dot(stack6(lower, 1, True), stack6(new, 0, False), 1, 0)
                for b in range(2):
                    w[b, pl.ds(at + 64, 64), :] = rest[64 * b : 64 * b + 64]
        here = (wide2 >= o) & (wide2 < o + 128)

        if t < 3:
            for b in range(2):
                s6[b] = stack6(v[b], 0, False)

        for i in range(t + 1, 4):
            rows = pl.ds(i * 128, 128)
            for b in range(2):
                lower = v[b, :, rows].T
                rest = jnp.where(here, 0.0, w[b, rows, :])
                w[b, rows, :] = rest - dot(stack6(lower, 1, True), s6[b], 1, 0)


def solve(x, ys, b):
    half = x.shape[1] // 2
    out = []
    for lo, depth in ((0, half), (half, 2 * half)):
        acc = None
        for y in ys:
            term = dot(x[:, :depth], y[b, lo : lo + half, :depth], 1, 1)
            acc = term if acc is None else acc + term
        out.append(acc)
    return jnp.concatenate(out, axis=1)


def panel_kernel(panel, diag, trail, cols_out, rows_out, own_out, trail_out, cols, rows, w, v, s6, hi, mid, lo, full, in_sems, *sems):
    fetch = pltpu.make_async_copy(diag, w, in_sems.at[0])
    fetch.start()
    gather = Gather(panel, cols, rows, *sems)
    gather.barrier()
    gather.start()
    fetch_trail = pltpu.make_async_copy(trail, trail_out, in_sems.at[1])
    fetch_trail.start()
    fetch.wait()

    def point(t, s, p):
        gather.point((2 * t + s) * 8 + p)

    factor(w, v, s6, point)
    ys = (hi, mid, lo)
    for b in range(2):
        hi[b], mid[b], lo[b] = split3(w[b])

    def solve_cols(group):
        slots = [gather.slot(dx, dz) for dx, dz in group]
        for b in range(2):
            x = jnp.concatenate([cols[b, i] for i in slots], axis=0)
            x = solve(x, ys[:2], b).astype(BF)
            for n, i in enumerate(slots):
                cols_out[b, i] = x[48 * n : 48 * n + 48]

    def solve_rows():
        gather.wait_rows()
        for b in range(2):
            full[b] = solve(jnp.concatenate([rows[b, i] for i in range(NC)], axis=0), ys, b)
            for i in range(NC):
                rows_out[b, i] = full[b, 48 * i : 48 * i + 48].astype(BF)
            own_out[b] = full[b, pl.ds(pl.multiple_of(gather.col * 48, 16), 48)]

    done = [e for h in sorted(PLAN) if h < LAST for e in PLAN[h]]
    late = list(PLAN.get(LAST, ()))
    ready = [e[1:] for e in done if ("A",) + e[1:] in done and e[0] == "B"]
    solve_rows()
    while late or ready:
        while late and (len(ready) < 8 or len(late) > 3 * len(ready)):
            event = late.pop(0)
            gather.arrival(*event)
            done.append(event)
            if ("A",) + event[1:] in done and ("B",) + event[1:] in done:
                ready.append(event[1:])
        solve_cols(ready[:8])
        ready = ready[8:]
    gather.drain()
    fetch_trail.wait()


def panel_step(panel, diagonal, trailing):
    nb, count, k = panel.shape
    vmem = pl.BlockSpec(memory_space=pltpu.VMEM)
    hbm = pl.BlockSpec(memory_space=pltpu.HBM)
    return pl.pallas_call(
        panel_kernel,
        in_specs=[hbm] * 3,
        out_specs=[vmem] * 4,
        out_shape=[
            jax.ShapeDtypeStruct((nb, NX * NZ, count, k), BF),
            jax.ShapeDtypeStruct((nb, NC, count, k), BF),
            jax.ShapeDtypeStruct(panel.shape, F32),
            jax.ShapeDtypeStruct(trailing.shape, F32),
        ],
        scratch_shapes=[
            pltpu.VMEM((nb, NX * NZ, count, k), BF),
            pltpu.VMEM((nb, NC, count, k), BF),
            pltpu.VMEM(diagonal.shape, F32),
            pltpu.VMEM((nb, 128, k), F32),
            pltpu.VMEM((nb, 768, k), BF),
            pltpu.VMEM(diagonal.shape, BF),
            pltpu.VMEM(diagonal.shape, BF),
            pltpu.VMEM(diagonal.shape, BF),
            pltpu.VMEM((nb, NC * count, k), F32),
            DMA((2,)),
        ] + GATHER_SEMS,
        compiler_params=pltpu.CompilerParams(
            collective_id=0, has_side_effects=True, vmem_limit_bytes=42 << 20
        ),
        cost_estimate=pl.CostEstimate(flops=10**10, bytes_accessed=10**7, transcendentals=0),
        name="panel_step",
    )(*(pltpu.with_memory_space_constraint(a, pltpu.HBM) for a in (panel, diagonal, trailing)))


WIDE = 512


def update_kernel(pat, cols, rows, own, trail, out, solved, buf, own_buf, sems, own_sem):
    row, col = lax.axis_index("row"), lax.axis_index("col")
    nb, m, n = buf.shape
    count = own.shape[1]
    first = (row * NC + col) * count
    low, high = first // BLK, (first + count - 1) // BLK
    at = first + lax.broadcasted_iota(jnp.int32, own.shape[1:], 0)
    keep = jnp.where(at < high * BLK, pat[low], pat[high]).astype(F32)
    for b in range(nb):
        own_buf[b] = own[b] * keep
    own_copy = pltpu.make_async_copy(own_buf, solved, own_sem)
    own_copy.start()
    keep_rows = [pat[row * (m // BLK) + i] for i in range(m // BLK)]
    copies = []
    for b in range(nb):
        for j in range(n // WIDE):
            there = pl.ds(j * WIDE, WIDE)
            prod = dot(rows[b], cols[b, there], 1, 1)
            for q in range(WIDE // BLK):
                keep_col = pat[col * (n // BLK) + j * (WIDE // BLK) + q]
                for i, keep_row in enumerate(keep_rows):
                    r = slice(i * BLK, (i + 1) * BLK)
                    c = slice(j * WIDE + q * BLK, j * WIDE + (q + 1) * BLK)
                    both = (keep_col * keep_row).astype(F32)
                    buf[b, r, c] = trail[b, r, c] - both * prod[r, q * BLK : (q + 1) * BLK]
            copy = pltpu.make_async_copy(buf.at[b, :, there], out.at[b, :, there], sems.at[b, j])
            copy.start()
            copies.append(copy)
    for copy in copies:
        copy.wait()
    own_copy.wait()


def update(pattern, cols, rows, own, trailing):
    vmem = pl.BlockSpec(memory_space=pltpu.VMEM)
    hbm = pl.BlockSpec(memory_space=pltpu.HBM)
    nb, m, n = trailing.shape
    return pl.pallas_call(
        update_kernel,
        in_specs=[pl.BlockSpec(memory_space=pltpu.SMEM)] + [vmem] * 4,
        out_specs=[hbm] * 2,
        out_shape=[jax.ShapeDtypeStruct(trailing.shape, F32), jax.ShapeDtypeStruct(own.shape, F32)],
        scratch_shapes=[
            pltpu.VMEM(trailing.shape, F32),
            pltpu.VMEM(own.shape, F32),
            DMA((nb, n // WIDE)),
            DMA,
        ],
        compiler_params=pltpu.CompilerParams(vmem_limit_bytes=36 << 20),
        cost_estimate=pl.CostEstimate(flops=10**9, bytes_accessed=10**7, transcendentals=0),
        name="update",
    )(pattern, cols, rows, own, trailing)


def per_device(trailing, panel, diagonal, pattern):
    cols, rows, own, trail = panel_step(panel, diagonal, trailing)
    nb, _, _, k = cols.shape
    return tuple(update(pattern, cols.reshape(nb, -1, k), rows.reshape(nb, -1, k), own, trail))


def solution(mesh):
    return jax.shard_map(
        per_device,
        mesh=mesh,
        in_specs=(P(None, "row", "col"), P(None, ("row", "col"), None), P(), P()),
        out_specs=(P(None, "row", "col"), P(None, ("row", "col"), None)),
        check_vma=False,
    )
```
